256 devices in a mesh: context: 64 (over x, z_hi, y, core), tensor: 4 (over z_lo).
Axes of the slice: x: 4, y: 4, z: 8 (z_hi: 2, z_lo: 4; z = z_hi * 4 + z_lo), core: 2. Of those that a mesh axis runs over, the one named last changes fastest.
Arguments:
- hidden_in: bfloat16 [32768, 4096], P(('context', 'tensor')), may hold values from -3 to 3
- norm_gain: float32 [4096], replicated, as said below
- w_query: bfloat16 [4096, 2048], P(None, 'tensor'), may hold values from -0.09375 to 0.09375
- w_key: bfloat16 [4096, 512], P(None, 'tensor'), may hold values from -0.09375 to 0.09375
- w_value: bfloat16 [4096, 512], P(None, 'tensor'), may hold values from -0.09375 to 0.09375
- w_out: bfloat16 [2048, 4096], P('tensor'), may hold values from -0.75 to 0.75
- offsets: int32 [64], replicated, may hold values from 0 to 127
Outputs:
- hidden_out: bfloat16 [32768, 4096], P(('context', 'tensor'))
The draws below stay inside these ranges and needn't reach their ends.
Inputs may be any that keep to these rules, and one draw needn't show every extreme that they name: `norm_gain`: gains of order one, all positive.
All inputs are finite; a program needn't handle non-finite values.
Results may differ from the reference program's by a relative error of at most 0.025.
Values may be sent and summed in bfloat16 or wider, within the bound.
A program may use at most 64 MiB of HBM per device.

```python
import jax
import jax.numpy as jnp
from jax import lax

D = 4096
HEADS = 16
KV_HEADS = 4
HD = 128
BLK = 512
TOKENS = 32768
N_CONTEXT = 64
N_TENSOR = 4


def draw_norm_gain(key, part):
    key = jax.random.fold_in(key, 7)
    return jax.random.uniform(key, (D,), jnp.float32, 0.5, 1.5)


def place_ends(array, rng, low, top_value):
    longest = array.shape.index(max(array.shape))
    spots = []
    for shift in (0, 1):
        where = [jax.random.randint(jax.random.fold_in(rng, axis), (), 0, length) for axis, length in enumerate(array.shape)]
        where[longest] = (where[longest] + shift) % array.shape[longest]
        spots.append(tuple(where))
    return array.at[spots[0]].set(low).at[spots[1]].set(top_value)


def levels(key, shape, cuts, least, largest):
    def one(axis_at, parts):
        draws = jax.random.uniform(jax.random.fold_in(jax.random.fold_in(key, 6), axis_at), (parts,), jnp.float32, least / len(cuts), largest / len(cuts))
        return jnp.repeat(jnp.exp(draws), shape[axis_at] // parts).reshape((-1,) + (1,) * (len(shape) - axis_at - 1))

    gain = one(*cuts[0])
    for cut in cuts[1:]:
        gain = gain * one(*cut)
    return gain


def centred(stream_key, extent, scale, bound, split=(), kind=jnp.bfloat16):
    array = jax.random.normal(stream_key, extent, jnp.float32) * scale
    if len(split) > 0:
        array = levels(stream_key, extent, split, -0.22, 0.18) * array
    return jnp.clip(array, min=-bound, max=bound).astype(kind)


def setup_inputs(seed: int = 0) -> dict:
    key_list = jax.random.split(jax.random.key(seed), 8)
    return {
        "hidden_in": centred(key_list[0], (TOKENS, D), 0.5, 3.0, ((0, 256),)),
        "norm_gain": draw_norm_gain(jax.random.fold_in(key_list[7], 71), 0),
        "w_query": centred(key_list[2], (D, HEADS * HD), D ** -0.5, 0.09375, ((1, 4),)),
        "w_key": centred(key_list[3], (D, KV_HEADS * HD), D ** -0.5, 0.09375, ((1, 4),)),
        "w_value": centred(key_list[4], (D, KV_HEADS * HD), D ** -0.5, 0.09375, ((1, 4),)),
        "w_out": centred(key_list[5], (HEADS * HD, D), (HEADS * HD // 32) ** -0.5, 0.75, ((0, 4),)),
        "offsets": place_ends(jax.random.randint(key_list[6], (N_CONTEXT,), 0, 128), jax.random.fold_in(key_list[6], 1), 0, 127).astype(jnp.int32),
    }


def rms_norm(rows_in, norm_gain):
    values = rows_in.astype(jnp.float32)
    mean_sq = lax.optimization_barrier(jnp.mean(values * values, axis=-1, keepdims=True))
    return (values * lax.rsqrt(mean_sq + 1e-05) * norm_gain).astype(jnp.bfloat16)

def rope_apply(values, positions):
    half = values.shape[-1] // 2
    freq = 500000.0 ** (-(jnp.arange(half).astype(jnp.float32) * 2.0 / values.shape[-1]))
    angle = positions.astype(jnp.float32)[:, None] * freq[None, :]
    cosine = jnp.concatenate([jnp.cos(angle), jnp.cos(angle)], axis=-1)[:, None, :]
    sine = jnp.concatenate([jnp.sin(angle), jnp.sin(angle)], axis=-1)[:, None, :]
    turned = jnp.concatenate([-values[..., half:], values[..., :half]], axis=-1)
    return values * cosine + turned * sine

def reference(hidden_in, norm_gain, w_query, w_key, w_value, w_out, offsets):
    anchor_norm = rms_norm(hidden_in[:BLK], norm_gain)
    base_pos = jnp.arange(BLK).astype(jnp.int32)
    anchor_pos = offsets[0] * BLK + base_pos
    anchor_key = rope_apply(jnp.dot(anchor_norm, w_key, preferred_element_type=jnp.float32).reshape(BLK, KV_HEADS, HD), anchor_pos).astype(jnp.bfloat16)
    anchor_value = jnp.dot(anchor_norm, w_value, preferred_element_type=jnp.float32).astype(jnp.bfloat16).reshape(BLK, KV_HEADS, HD)
    group_size = HEADS // KV_HEADS
    causal = base_pos[None, :] <= base_pos[:, None]
    neg = jnp.float32(-1e+30)
    share_cols = HEADS * HD // N_TENSOR

    def one_block(index):
        block_rows = lax.dynamic_slice_in_dim(hidden_in, index * BLK, BLK, 0)
        normed = rms_norm(block_rows, norm_gain)
        positions = offsets[index] * BLK + base_pos
        query = rope_apply(jnp.dot(normed, w_query, preferred_element_type=jnp.float32).reshape(BLK, HEADS, HD), positions).astype(jnp.bfloat16)
        own_key = rope_apply(jnp.dot(normed, w_key, preferred_element_type=jnp.float32).reshape(BLK, KV_HEADS, HD), positions).astype(jnp.bfloat16)
        own_value = jnp.dot(normed, w_value, preferred_element_type=jnp.float32).astype(jnp.bfloat16).reshape(BLK, KV_HEADS, HD)
        query_f = query.reshape(BLK, KV_HEADS, group_size, HD).astype(jnp.float32)
        scale = 1.0 / HD ** 0.5
        own_scores = jnp.einsum('qkgd,skd->kgqs', query_f, own_key.astype(jnp.float32)) * scale
        anchor_scores = jnp.einsum('qkgd,skd->kgqs', query_f, anchor_key.astype(jnp.float32)) * scale
        own_scores = jnp.where(causal, own_scores, neg)
        anchor_scores = jnp.where(index == 0, neg, anchor_scores)
        scores = jnp.concatenate([anchor_scores, own_scores], axis=-1)
        top = lax.optimization_barrier(jnp.max(scores, axis=-1, keepdims=True))
        expo = jnp.exp(scores - top)
        weights = (expo / lax.optimization_barrier(jnp.sum(expo, axis=-1, keepdims=True))).astype(jnp.bfloat16)
        values = jnp.concatenate([anchor_value, own_value], axis=0)
        attended = jnp.einsum('kgqs,skd->qkgd', weights.astype(jnp.float32), values.astype(jnp.float32))
        attended = attended.astype(jnp.bfloat16).reshape(BLK, HEADS * HD)
        branch = jnp.zeros((BLK, D), jnp.float32)
        for shard in range(N_TENSOR):
            part_cols = attended[:, shard * share_cols:(shard + 1) * share_cols]
            part_rows = w_out[shard * share_cols:(shard + 1) * share_cols]
            share = jnp.dot(part_cols, part_rows, preferred_element_type=jnp.float32).astype(jnp.bfloat16)
            share = lax.optimization_barrier(share)
            branch = branch + share.astype(jnp.float32)
        return (block_rows.astype(jnp.float32) + branch).astype(jnp.bfloat16)
    result = lax.map(one_block, jnp.arange(N_CONTEXT).astype(jnp.int32))
    return result.reshape(TOKENS, D)
```

```python
import functools

import jax
import jax.numpy as jnp
from jax import lax
from jax.experimental import pallas as pl
from jax.experimental.pallas import tpu as pltpu
from jax.sharding import PartitionSpec as P

HD = 128
EPS = 1e-05
NEG = -1e30
MESH = pl.DeviceIdType.MESH
F32 = jnp.float32
BF16 = jnp.bfloat16
N_SEM = 96


def kernel(
    x_ref, gain_ref, cos_ref, sin_ref, wq_hbm, wk_hbm, wv_hbm, wo_hbm, out_ref,
    w_q, w_kv, w_o, normed, grain, grain_norm, anchor_kv, own_kv, q_buf, att, send_buf, recv_buf, partial,
    ss, rs, ls,
):
    ctx = lax.axis_index("context")
    t = lax.axis_index("tensor")
    core = ctx % 2
    y = (ctx // 2) % 4
    zh = (ctx // 8) % 2
    x = ctx // 16
    a = x * (1 - core) + y * core
    b = y * (1 - core) + x * core
    m = b * 4 + a
    mine = core * 16 + m
    slot = t // 2
    other = 1 - slot
    parity = t % 2

    def at(x_, y_, zh_, t_, core_):
        return (((x_ * 2 + zh_) * 4 + y_) * 2 + core_, t_)

    def ring_a(d):
        return at((x + d * (1 - core)) % 4, (y + d * core) % 4, zh, t, core)

    def ring_b(d):
        return at((x + d * core) % 4, (y + d * (1 - core)) % 4, zh, t, core)

    sibling = at(x, y, zh, t, 1 - core)
    pair = at(x, y, zh, t + 1 - 2 * parity, core)
    outer = (t // 2 + t) % 2
    wpart = at(x, y, (zh + 1 - outer) % 2, 3 - t, core)
    mirror = at(x, y, zh, 3 - t, core)
    same_type = [at(x, y, 1 - zh, t, core), at(x, y, zh, 3 - t, core), at(x, y, 1 - zh, 3 - t, core)]

    count = [0]
    sends = []

    def sem():
        count[0] += 1
        return count[0] - 1

    def send(k, src, dst, dev, keep=True):
        cp = pltpu.make_async_remote_copy(
            src_ref=src, dst_ref=dst, send_sem=ss.at[k], recv_sem=rs.at[k], device_id=dev, device_id_type=MESH
        )
        cp.start()
        if keep:
            sends.append(cp)
        return cp

    def recv(k, dst, dev):
        pltpu.make_async_remote_copy(
            src_ref=dst, dst_ref=dst, send_sem=ss.at[k], recv_sem=rs.at[k], device_id=dev, device_id_type=MESH
        ).wait_recv()

    is_source = ctx == 0
    takes = (zh == 0) & (core == slot)
    takes_first = takes & (m // 8 == parity)
    takes_second = takes & (m // 8 != parity)
    self_grain = is_source & (t == 0)

    bar = pltpu.get_barrier_semaphore()
    peers = [ring_a(d) for d in (1, 2, 3)] + [ring_b(d) for d in (1, 2, 3)] + [sibling, pair] + same_type
    for p in peers:
        pl.semaphore_signal(bar, inc=1, device_id=p, device_id_type=MESH)

    @pl.when(takes_first & jnp.logical_not(self_grain))
    def _():
        pl.semaphore_signal(bar, inc=1, device_id=(0, t), device_id_type=MESH)

    loads = []
    for i, (src, dst) in enumerate(
        [
            (wk_hbm, w_kv.at[slot, :, pl.ds(0, 128)]),
            (wv_hbm, w_kv.at[slot, :, pl.ds(128, 128)]),
            (wq_hbm, w_q.at[slot]),
            (wo_hbm, w_o.at[slot]),
        ]
    ):
        cp = pltpu.make_async_copy(src, dst, ls.at[i])
        cp.start()
        loads.append(cp)

    grains_out = jnp.where(is_source, jnp.where(t == 0, 7, 8), 0)
    pl.semaphore_wait(bar, len(peers) + grains_out)

    k_scat = [sem() for _ in range(8)]

    def grain_target(j):
        mm = 8 * parity + j
        aa = mm % 4
        bb = mm // 4
        return at(aa * (1 - slot) + bb * slot, bb * (1 - slot) + aa * slot, 0, t, slot)

    def grain_copy(j):
        return pltpu.make_async_remote_copy(
            src_ref=x_ref.at[pl.ds(16 * j, 16)], dst_ref=grain, send_sem=ss.at[k_scat[j]], recv_sem=rs.at[k_scat[0]],
            device_id=grain_target(j), device_id_type=MESH,
        )

    @pl.when(is_source)
    def _():
        for j in range(1, 8):
            grain_copy(j).start()

    @pl.when(is_source & (t != 0))
    def _():
        grain_copy(0).start()

    @pl.when(self_grain)
    def _():
        cp = pltpu.make_async_copy(x_ref.at[pl.ds(0, 16)], grain, ls.at[4])
        cp.start()
        cp.wait()

    def kv_view(start, n):
        return w_kv.at[other, pl.ds(pl.multiple_of(start * 128, 128), n * 128)]

    def q_view(start, n):
        return w_q.at[other, pl.ds(pl.multiple_of(start * 128, 128), n * 128)]

    def o_view(start, n):
        return w_o.at[other, pl.ds(pl.multiple_of(start * 16, 16), n * 16)]

    def anchor_view(start, n):
        return anchor_kv.at[:, pl.ds(pl.multiple_of(start * 16, 16), n * 16)]

    rows128 = pl.ds(pl.multiple_of(mine * 128, 128), 128)
    rows16 = pl.ds(pl.multiple_of(mine * 16, 16), 16)
    k_zk, k_zv, k_zq, k_zo = sem(), sem(), sem(), sem()
    send(k_zk, wk_hbm.at[rows128], w_kv.at[slot, rows128, pl.ds(0, 128)], wpart)
    send(k_zv, wv_hbm.at[rows128], w_kv.at[slot, rows128, pl.ds(128, 128)], wpart)
    send(k_zq, wq_hbm.at[rows128], w_q.at[slot, rows128], wpart)
    send(k_zo, wo_hbm.at[rows16], w_o.at[slot, rows16], wpart)

    class Gather:
        def __init__(self, view):
            self.view = view
            self.ka = [sem() for _ in range(3)]
            self.kb = [sem() for _ in range(3)]
            self.kd = [sem() for _ in range(4)]

        def send_a(self):
            v = self.view(mine, 1)
            for d in (1, 3, 2):
                send(self.ka[d - 1], v, v, ring_a(d))

        def wait_a(self):
            for d in (1, 3, 2):
                recv(self.ka[d - 1], self.view(core * 16 + b * 4 + (a + 4 - d) % 4, 1), ring_a(4 - d))

        def send_b(self):
            v = self.view(core * 16 + b * 4, 4)
            for d in (1, 3, 2):
                send(self.kb[d - 1], v, v, ring_b(d))
            send(self.kd[0], v, v, sibling)

        def wait_b(self):
            for d in (1, 3, 2):
                v = self.view(core * 16 + ((b + 4 - d) % 4) * 4, 4)
                recv(self.kb[d - 1], v, ring_b(4 - d))
                send(self.kd[d], v, v, sibling)

        def wait_d(self):
            for d in (0, 1, 3, 2):
                recv(self.kd[d], self.view((1 - core) * 16 + ((a + 4 - d) % 4) * 4, 4), sibling)

    kv_gather, q_gather, o_gather, an_gather = (Gather(v) for v in (kv_view, q_view, o_view, anchor_view))

    def norm(rows):
        v = rows.astype(F32)
        mean_sq = jnp.mean(v * v, axis=-1, keepdims=True)
        return (v * lax.rsqrt(mean_sq + EPS) * gain_ref[...]).astype(BF16)

    my_half = parity
    k_norm = [sem() for _ in range(4)]

    for i in range(4):

        @pl.loop(0, 2)
        def _(r, i=i):
            rr = pl.ds(pl.multiple_of(i * 32 + r * 16, 16), 16)
            normed[my_half, rr] = norm(x_ref[rr])

        v = normed.at[my_half, pl.ds(i * 32, 32)]
        send(k_norm[i], v, v, pair)

    recv(k_zk, w_kv.at[other, rows128, pl.ds(0, 128)], wpart)
    recv(k_zv, w_kv.at[other, rows128, pl.ds(128, 128)], wpart)
    kv_gather.send_a()

    k_pair = sem()

    def grain_forward():
        return pltpu.make_async_remote_copy(
            src_ref=grain, dst_ref=grain, send_sem=ss.at[k_pair], recv_sem=rs.at[k_pair], device_id=pair, device_id_type=MESH
        )

    @pl.when(takes_first & jnp.logical_not(self_grain))
    def _():
        recv(k_scat[0], grain, (0, t))

    @pl.when(takes_first)
    def _():
        grain_forward().start()

    kv_gather.wait_a()
    kv_gather.send_b()
    recv(k_zq, w_q.at[other, rows128], wpart)
    q_gather.send_a()
    kv_gather.wait_b()
    q_gather.wait_a()
    q_gather.send_b()
    recv(k_zo, w_o.at[other, rows16], wpart)
    o_gather.send_a()
    for cp in loads:
        cp.wait()
    kv_gather.wait_d()

    def rope(v, c, s):
        return v * c + pltpu.roll(v, 64, 1) * s

    k_an = [sem() for _ in range(3)]
    an_mine = anchor_view(mine, 1)

    def anchor_copy(i):
        return pltpu.make_async_remote_copy(
            src_ref=an_mine, dst_ref=an_mine, send_sem=ss.at[k_an[i]], recv_sem=rs.at[k_an[0]],
            device_id=same_type[i], device_id_type=MESH,
        )

    @pl.when(takes_second)
    def _():
        recv(k_pair, grain, pair)

    @pl.when(takes)
    def _():
        grain_norm[...] = norm(grain[...])
        c = cos_ref[pl.ds(256, 16)]
        s = sin_ref[pl.ds(256, 16)]
        for i in range(2):
            kv = jnp.dot(grain_norm[...], w_kv[i], preferred_element_type=F32)
            anchor_kv[i, rows16, pl.ds(0, 128)] = rope(kv[:, :128], c, s).astype(BF16)
            anchor_kv[i, rows16, pl.ds(128, 128)] = kv[:, 128:].astype(BF16)
        for i in range(3):
            anchor_copy(i).start()

    def kv_rows(half, start, n):
        rows = pl.ds(start, n)
        table = pl.ds(pl.multiple_of(half * 128 + start, 16), n)
        c = cos_ref[table]
        s = sin_ref[table]
        place = pl.ds(pl.multiple_of((slot * 2 + half) * 128 + start, 16), n)
        for i in range(2):
            kv = jnp.dot(normed[half, rows], w_kv[i], preferred_element_type=F32)
            own_kv[i, place, pl.ds(0, 128)] = rope(kv[:, :128], c, s).astype(BF16)
            own_kv[i, place, pl.ds(128, 128)] = kv[:, 128:].astype(BF16)

    k_kv = [sem() for _ in range(5)]

    def kv_copy(k, half, start, n):
        v = own_kv.at[:, pl.ds(pl.multiple_of(half * 128 + start, 16), n)]
        return pltpu.make_async_remote_copy(
            src_ref=v, dst_ref=v, send_sem=ss.at[k], recv_sem=rs.at[k], device_id=mirror, device_id_type=MESH
        )

    kv_rows(my_half, 0, 128)
    lower = slot == 0

    @pl.when(lower)
    def _():
        kv_copy(k_kv[0], my_half, 0, 128).start()
        own_kv[:, pl.ds(256, 256)] = jnp.zeros((2, 256, 256), BF16)

    @pl.when(jnp.logical_not(takes))
    def _():
        recv(k_an[0], an_mine, pair)

    an_gather.send_a()

    def q_rows(half, i):
        table = pl.ds(pl.multiple_of(half * 128, 128), 128)

        @pl.loop(0, 2)
        def _(j):
            c = cos_ref[table]
            s = sin_ref[table]
            q = jnp.dot(
                normed[half], w_q[i, :, pl.ds(pl.multiple_of(j * 256, 256), 256)], preferred_element_type=F32
            )
            for h in range(2):
                q_buf[half, i, j * 2 + h] = rope(q[:, h * 128 : (h + 1) * 128], c, s).astype(BF16)

    q_rows(my_half, slot)
    an_gather.wait_a()
    an_gather.send_b()
    q_gather.wait_b()
    o_gather.wait_a()
    o_gather.send_b()
    an_gather.wait_b()
    q_gather.wait_d()
    q_rows(my_half, other)

    far = 1 - my_half
    for i in range(4):
        recv(k_norm[i], normed.at[far, pl.ds(i * 32, 32)], pair)
        kv_rows(far, i * 32, 32)

        @pl.when(lower)
        def _(i=i):
            kv_copy(k_kv[1 + i], far, i * 32, 32).start()

    q_rows(far, slot)
    q_rows(far, other)
    an_gather.wait_d()
    o_gather.wait_b()

    @pl.when(jnp.logical_not(lower))
    def _():
        kv_copy(k_kv[0], 1 - my_half, 0, 128).wait_recv()
        for i in range(4):
            kv_copy(k_kv[1 + i], my_half, i * 32, 32).wait_recv()

    scale = 1.0 / HD**0.5
    first_group = ctx == 0

    def attend(half):
        @pl.loop(0, 8)
        def _(h):
            i = h // 4
            q = q_buf[half, i, h % 4]
            dims = (((1,), (1,)), ((), ()))
            s1 = lax.dot_general(q, anchor_kv[i, :, pl.ds(0, 128)], dims, preferred_element_type=F32)
            s2 = lax.dot_general(q, own_kv[i, :, pl.ds(0, 128)], dims, preferred_element_type=F32)
            qpos = (slot * 2 + half) * 128 + lax.broadcasted_iota(jnp.int32, (128, 512), 0)
            kpos = lax.broadcasted_iota(jnp.int32, (128, 512), 1)
            s1 = jnp.where(first_group, NEG, s1 * scale)
            s2 = jnp.where(kpos <= qpos, s2 * scale, NEG)
            top = jnp.maximum(jnp.max(s1, axis=-1, keepdims=True), jnp.max(s2, axis=-1, keepdims=True))
            e1 = jnp.exp(s1 - top)
            e2 = jnp.exp(s2 - top)
            total = jnp.sum(e1, axis=-1, keepdims=True) + jnp.sum(e2, axis=-1, keepdims=True)
            o = jnp.dot(e1.astype(BF16), anchor_kv[i, :, pl.ds(128, 128)], preferred_element_type=F32)
            o += jnp.dot(e2.astype(BF16), own_kv[i, :, pl.ds(128, 128)], preferred_element_type=F32)
            att[half, i, :, pl.ds(pl.multiple_of((h % 4) * 128, 128), 128)] = (o / total).astype(BF16)

    def out_cols(half, start, n):
        cols = pl.ds(pl.multiple_of(start, 256), n)
        return jnp.dot(att[half, 0], w_o[0, :, cols], preferred_element_type=F32) + jnp.dot(
            att[half, 1], w_o[1, :, cols], preferred_element_type=F32
        )

    attend(far)
    o_gather.wait_d()
    k_sum = [sem() for _ in range(4)]
    for i in range(4):

        @pl.loop(0, 4)
        def _(j, i=i):
            send_buf[i, :, pl.ds(pl.multiple_of(j * 256, 256), 256)] = out_cols(far, i * 1024 + j * 256, 256).astype(BF16)

        send(k_sum[i], send_buf.at[i], recv_buf.at[i], pair)

    attend(my_half)

    @pl.loop(0, 16)
    def _(j):
        cols = pl.ds(pl.multiple_of(j * 256, 256), 256)
        partial[:, cols] = x_ref[:, cols].astype(F32) + out_cols(my_half, j * 256, 256)

    @pl.when(is_source)
    def _():
        for j in range(1, 8):
            grain_copy(j).wait_send()

    @pl.when(is_source & (t != 0))
    def _():
        grain_copy(0).wait_send()

    @pl.when(takes_first)
    def _():
        grain_forward().wait_send()

    @pl.when(takes)
    def _():
        for i in range(3):
            anchor_copy(i).wait_send()

    @pl.when(lower)
    def _():
        kv_copy(k_kv[0], my_half, 0, 128).wait_send()
        for i in range(4):
            kv_copy(k_kv[1 + i], far, i * 32, 32).wait_send()

    for cp in sends[:-4]:
        cp.wait_send()
    for i in range(4):
        recv(k_sum[i], recv_buf.at[i], pair)

        @pl.loop(0, 4)
        def _(j, i=i):
            cols = pl.ds(pl.multiple_of(i * 1024 + j * 256, 256), 256)
            got = recv_buf[i, :, pl.ds(pl.multiple_of(j * 256, 256), 256)].astype(F32)
            out_ref[:, cols] = (partial[:, cols] + got).astype(BF16)

    for cp in sends[-4:]:
        cp.wait_send()
    assert count[0] <= N_SEM, count[0]


def tables(offsets):
    ctx = lax.axis_index("context")
    t = lax.axis_index("tensor")
    core = ctx % 2
    y = (ctx // 2) % 4
    x = ctx // 16
    a = x * (1 - core) + y * core
    b = y * (1 - core) + x * core
    rows = jnp.arange(272)
    own = offsets[ctx] * 512 + (t // 2) * 256 + rows
    anchor = offsets[0] * 512 + (core * 16 + b * 4 + a) * 16 + rows - 256
    positions = jnp.where(rows < 256, own, anchor).astype(F32)
    half = HD // 2
    freq = 500000.0 ** (-(jnp.arange(half).astype(F32) * 2.0 / HD))
    angle = positions[:, None] * freq[None, :]
    c = jnp.cos(angle)
    s = jnp.sin(angle)
    return jnp.concatenate([c, c], axis=-1), jnp.concatenate([-s, s], axis=-1)


def body(hidden_in, norm_gain, w_query, w_key, w_value, w_out, offsets):
    cosine, sine = tables(offsets)
    vmem = pl.BlockSpec(memory_space=pltpu.VMEM)
    hbm = pl.BlockSpec(memory_space=pl.ANY)
    return pl.pallas_call(
        kernel,
        out_shape=jax.ShapeDtypeStruct((128, 4096), BF16),
        in_specs=[vmem] * 4 + [hbm] * 4,
        out_specs=vmem,
        scratch_shapes=[
            pltpu.VMEM((2, 4096, 512), BF16),
            pltpu.VMEM((2, 4096, 256), BF16),
            pltpu.VMEM((2, 512, 4096), BF16),
            pltpu.VMEM((2, 128, 4096), BF16),
            pltpu.VMEM((16, 4096), BF16),
            pltpu.VMEM((16, 4096), BF16),
            pltpu.VMEM((2, 512, 256), BF16),
            pltpu.VMEM((2, 512, 256), BF16),
            pltpu.VMEM((2, 2, 4, 128, 128), BF16),
            pltpu.VMEM((2, 2, 128, 512), BF16),
            pltpu.VMEM((4, 128, 1024), BF16),
            pltpu.VMEM((4, 128, 1024), BF16),
            pltpu.VMEM((128, 4096), F32),
            pltpu.SemaphoreType.DMA((N_SEM,)),
            pltpu.SemaphoreType.DMA((N_SEM,)),
            pltpu.SemaphoreType.DMA((5,)),
        ],
        compiler_params=pltpu.CompilerParams(collective_id=0, has_side_effects=True, vmem_limit_bytes=56 * 2**20),
        cost_estimate=pl.CostEstimate(flops=10**10, bytes_accessed=2 * 10**7, transcendentals=2 * 10**6),
    )(hidden_in, norm_gain.reshape(1, 4096), cosine, sine, w_query, w_key, w_value, w_out)


def solution(mesh):
    placed = (
        P(("context", "tensor"), None),
        P(),
        P(None, "tensor"),
        P(None, "tensor"),
        P(None, "tensor"),
        P("tensor", None),
        P(),
    )
    return jax.shard_map(
        body, mesh=mesh, in_specs=placed, out_specs=P(("context", "tensor"), None), check_vma=False
    )
```

```python
import jax
import jax.numpy as jnp
import numpy as np
from jax import lax
from jax.experimental import pallas as pl
from jax.experimental.pallas import tpu as pltpu
from jax.sharding import PartitionSpec as P

HD = 128
EPS = 1e-05
NEG = -1e30
MESH = pl.DeviceIdType.MESH
F32 = jnp.float32
BF16 = jnp.bfloat16
N_SEM = 144


def kernel(
    offsets_ref, x_ref, gain_ref, base_cos, base_sin, row_cos, row_sin, wq_hbm, wk_hbm, wv_hbm, wo_hbm, out_ref,
    w_q, w_kv, w_o, normed, grain, grain_norm, anchor_kv, block_kv, q_own, q_near, att_own, att_near, send_buf, recv_buf,
    partial, cos_ref, sin_ref, ss, rs, ls,
):
    ctx = lax.axis_index("context")
    t = lax.axis_index("tensor")
    core = ctx % 2
    y = (ctx // 2) % 4
    zh = (ctx // 8) % 2
    x = ctx // 16
    a = x * (1 - core) + y * core
    b = y * (1 - core) + x * core
    m = b * 4 + a
    mine = core * 16 + m
    slot = t // 2
    other = 1 - slot
    parity = t % 2

    def at(x_, y_, zh_, t_, core_):
        return (((x_ * 2 + zh_) * 4 + y_) * 2 + core_, t_)

    def ring_a(d):
        return at((x + d * (1 - core)) % 4, (y + d * core) % 4, zh, t, core)

    def ring_b(d):
        return at((x + d * core) % 4, (y + d * (1 - core)) % 4, zh, t, core)

    def along_z(d):
        z = (zh * 4 + t + d) % 8
        return at(x, y, z // 4, z % 4, core)

    sibling = at(x, y, zh, t, 1 - core)
    above, below = along_z(1), along_z(7)
    pair = at(x, y, zh, t + 1 - 2 * parity, core)
    wpart = at(x, y, (zh + core) % 2, (t + 2) % 4, core)
    same_type = [along_z(2), along_z(4), along_z(6)]
    foreign = ctx + 8 - 16 * zh
    low_foreign = jnp.where(t == 0, 1, 0)
    high_foreign = jnp.where(t == 3, 1, 0)
    low_ctx = ctx + (foreign - ctx) * low_foreign
    high_ctx = ctx + (foreign - ctx) * high_foreign
    own_start = t * 128
    low_start = (t * 128 + 448) % 512
    high_start = (t * 128 + 128) % 512

    count = [0]
    sends = []

    def sem():
        count[0] += 1
        return count[0] - 1

    def send(k, src, dst, dev, keep=True):
        cp = pltpu.make_async_remote_copy(
            src_ref=src, dst_ref=dst, send_sem=ss.at[k], recv_sem=rs.at[k], device_id=dev, device_id_type=MESH
        )
        cp.start()
        if keep:
            sends.append(cp)
        return cp

    def recv(k, dst, dev):
        pltpu.make_async_remote_copy(
            src_ref=dst, dst_ref=dst, send_sem=ss.at[k], recv_sem=rs.at[k], device_id=dev, device_id_type=MESH
        ).wait_recv()

    is_source = ctx == 0
    takes = (zh == 0) & (core == slot)
    takes_first = takes & (m // 8 == parity)
    takes_second = takes & (m // 8 != parity)
    self_grain = is_source & (t == 0)

    bar = pltpu.get_barrier_semaphore()
    peers = [ring_a(d) for d in (1, 2, 3)] + [ring_b(d) for d in (1, 2, 3)] + [sibling, above, below] + same_type
    for p in peers:
        pl.semaphore_signal(bar, inc=1, device_id=p, device_id_type=MESH)

    @pl.when(takes_first & jnp.logical_not(self_grain))
    def _():
        pl.semaphore_signal(bar, inc=1, device_id=(0, t), device_id_type=MESH)

    loads = []
    for i, (src, dst) in enumerate(
        [
            (wk_hbm, w_kv.at[slot, :, pl.ds(0, 128)]),
            (wv_hbm, w_kv.at[slot, :, pl.ds(128, 128)]),
        ]
        + [(wq_hbm.at[pl.ds(j * 512, 512)], w_q.at[slot, j]) for j in range(8)]
        + [(wo_hbm.at[:, pl.ds(j * 512, 512)], w_o.at[slot, j]) for j in range(8)]
    ):
        cp = pltpu.make_async_copy(src, dst, ls.at[i])
        cp.start()
        loads.append(cp)

    def fill_tables(at_row, n, row, offset):
        cb = base_cos[pl.ds(offset, 1)]
        sb = base_sin[pl.ds(offset, 1)]
        cr = row_cos[pl.ds(row, n)]
        sr = row_sin[pl.ds(row, n)]
        cos_ref[pl.ds(at_row, n)] = cb * cr - sb * sr
        sin_ref[pl.ds(at_row, n)] = sb * cr + cb * sr

    fill_tables(0, 128, pl.multiple_of(own_start, 128), offsets_ref[ctx])
    fill_tables(128, 64, pl.multiple_of(low_start, 64), offsets_ref[low_ctx])
    fill_tables(192, 64, pl.multiple_of(high_start, 64), offsets_ref[high_ctx])
    fill_tables(256, 16, pl.multiple_of(mine * 16, 16), offsets_ref[0])

    grains_out = jnp.where(is_source, jnp.where(t == 0, 7, 8), 0)
    pl.semaphore_wait(bar, len(peers) + grains_out)

    rows128 = pl.ds(pl.multiple_of(mine * 128, 128), 128)
    rows16 = pl.ds(pl.multiple_of(mine * 16, 16), 16)
    my_block = core * 4 + b
    o_cols = pl.ds(pl.multiple_of(my_block * 512, 512), 512)
    quarter = pl.ds(pl.multiple_of(a * 128, 128), 128)
    k_zk, k_zv, k_zq, k_zo = sem(), sem(), sem(), sem()
    send(k_zk, wk_hbm.at[rows128], w_kv.at[slot, rows128, pl.ds(0, 128)], wpart)
    send(k_zv, wv_hbm.at[rows128], w_kv.at[slot, rows128, pl.ds(128, 128)], wpart)
    send(k_zq, wq_hbm.at[rows128], w_q.at[slot, my_block, quarter], wpart)

    k_scat = [sem() for _ in range(8)]

    def grain_target(j):
        mm = 8 * parity + j
        aa = mm % 4
        bb = mm // 4
        return at(aa * (1 - slot) + bb * slot, bb * (1 - slot) + aa * slot, 0, t, slot)

    def grain_copy(j):
        return pltpu.make_async_remote_copy(
            src_ref=x_ref.at[pl.ds(16 * j, 16)], dst_ref=grain, send_sem=ss.at[k_scat[j]], recv_sem=rs.at[k_scat[0]],
            device_id=grain_target(j), device_id_type=MESH,
        )

    @pl.when(is_source)
    def _():
        for j in range(1, 8):
            grain_copy(j).start()

    @pl.when(is_source & (t != 0))
    def _():
        grain_copy(0).start()

    @pl.when(self_grain)
    def _():
        cp = pltpu.make_async_copy(x_ref.at[pl.ds(0, 16)], grain, ls.at[18])
        cp.start()
        cp.wait()

    def kv_one(c_, b_, a_):
        return w_kv.at[other, pl.ds(pl.multiple_of((c_ * 16 + b_ * 4 + a_) * 128, 128), 128)]

    def kv_block(c_, b_):
        return w_kv.at[other, pl.ds(pl.multiple_of((c_ * 4 + b_) * 512, 512), 512)]

    def an_one(c_, b_, a_):
        return anchor_kv.at[:, pl.ds(pl.multiple_of((c_ * 16 + b_ * 4 + a_) * 16, 16), 16)]

    def an_block(c_, b_):
        return anchor_kv.at[:, pl.ds(pl.multiple_of((c_ * 4 + b_) * 64, 64), 64)]

    class Gather:
        def __init__(self, one, block):
            self.one, self.block = one, block
            self.ka = [sem() for _ in range(3)]
            self.kb = [sem() for _ in range(3)]
            self.kd = [sem() for _ in range(4)]

        def send_a(self):
            v = self.one(core, b, a)
            for d in (1, 3, 2):
                send(self.ka[d - 1], v, v, ring_a(d))

        def wait_a(self):
            for d in (1, 3, 2):
                recv(self.ka[d - 1], self.one(core, b, (a + 4 - d) % 4), ring_a(4 - d))

        def send_b(self):
            v = self.block(core, b)
            for d in (1, 3, 2):
                send(self.kb[d - 1], v, v, ring_b(d))
            send(self.kd[0], v, v, sibling)

        def wait_b(self):
            for d in (1, 3, 2):
                v = self.block(core, (b + 4 - d) % 4)
                recv(self.kb[d - 1], v, ring_b(4 - d))
                send(self.kd[d], v, v, sibling)

        def wait_d(self):
            for d in (0, 1, 3, 2):
                recv(self.kd[d], self.block(1 - core, (a + 4 - d) % 4), sibling)

    class Stream:
        def __init__(self, block, pieces, slices):
            self.block, self.n, self.g = block, pieces, 512 // pieces
            self.ka = [sem() for _ in range(3)] if slices else []
            self.kb = [[sem() for _ in range(2)] for _ in range(pieces)]
            self.kc = [[sem() for _ in range(2)] for _ in range(pieces)]
            self.kd = [[sem() for _ in range(4)] for _ in range(pieces)]

        def piece(self, c_, b_, k):
            return self.block(c_, b_, pl.ds(k * self.g, self.g))

        def half(self, b_, k, h):
            return self.block(core, b_, pl.ds(k * self.g + h * (self.g // 2), self.g // 2))

        def one(self, a_):
            return self.block(core, b, pl.ds(pl.multiple_of(a_ * 128, 128), 128))

        def send_a(self):
            v = self.one(a)
            for d in (1, 3, 2):
                send(self.ka[d - 1], v, v, ring_a(d))

        def wait_a(self):
            for d in (1, 3, 2):
                recv(self.ka[d - 1], self.one((a + 4 - d) % 4), ring_a(4 - d))

        def first(self, k):
            v = self.piece(core, b, k)
            for i, d in enumerate((1, 3)):
                send(self.kb[k][i], v, v, ring_b(d))
            send(self.kd[k][0], v, v, sibling)

        def on(self, k):
            for i, d in enumerate((1, 3)):
                near = (b + 4 - d) % 4
                recv(self.kb[k][i], self.piece(core, near, k), ring_b(4 - d))
                v = self.half(near, k, i)
                send(self.kc[k][i], v, v, ring_b(d))
                v = self.piece(core, near, k)
                send(self.kd[k][d], v, v, sibling)

        def last(self, k):
            far_b = (b + 2) % 4
            for i, d in enumerate((1, 3)):
                recv(self.kc[k][i], self.half(far_b, k, i), ring_b(4 - d))
            v = self.piece(core, far_b, k)
            send(self.kd[k][2], v, v, sibling)

        def wait_d(self, ds=(0, 1, 3, 2)):
            for d in ds:
                for k in range(self.n):
                    recv(self.kd[k][d], self.piece(1 - core, (a + 4 - d) % 4, k), sibling)

    def q_view(c_, b_, rows):
        return w_q.at[other, c_ * 4 + b_, rows]

    def o_view(c_, b_, rows):
        return w_o.at[other, c_ * 4 + b_, rows]

    kv_gather = Gather(kv_one, kv_block)
    an_gather = Gather(an_one, an_block)
    q_str = Stream(q_view, 2, True)
    o_str = Stream(o_view, 2, True)

    def norm(rows):
        v = rows.astype(F32)
        mean_sq = jnp.mean(v * v, axis=-1, keepdims=True)
        return (v * lax.rsqrt(mean_sq + EPS) * gain_ref[...]).astype(BF16)

    k_norm = [sem() for _ in range(2)]
    for i in range(2):

        @pl.loop(0, 4)
        def _(r, i=i):
            rr = pl.ds(pl.multiple_of(i * 64 + r * 16, 16), 16)
            normed[rr] = norm(x_ref[rr])

        if i == 0:
            send(k_norm[0], normed.at[pl.ds(0, 64)], normed.at[pl.ds(192, 64)], below)
        else:
            send(k_norm[1], normed.at[pl.ds(64, 64)], normed.at[pl.ds(128, 64)], above)

    recv(k_zk, w_kv.at[other, rows128, pl.ds(0, 128)], wpart)
    recv(k_zv, w_kv.at[other, rows128, pl.ds(128, 128)], wpart)
    kv_gather.send_a()

    k_pair = sem()

    def grain_forward():
        return pltpu.make_async_remote_copy(
            src_ref=grain, dst_ref=grain, send_sem=ss.at[k_pair], recv_sem=rs.at[k_pair], device_id=pair, device_id_type=MESH
        )

    @pl.when(takes_first & jnp.logical_not(self_grain))
    def _():
        recv(k_scat[0], grain, (0, t))

    @pl.when(takes_first)
    def _():
        grain_forward().start()

    recv(k_zq, q_str.one(a), wpart)
    q_str.send_a()
    kv_gather.wait_a()
    kv_gather.send_b()
    send(k_zo, wo_hbm.at[quarter, o_cols], w_o.at[slot, my_block, quarter], wpart)
    for cp in loads:
        cp.wait()

    def rope(v, c, s):
        return v * c + pltpu.roll(v, 64, 1) * s

    k_own = [sem() for _ in range(4)]
    k_low, k_high, k_high4 = sem(), sem(), sem()

    def kv_view(buf, i, start, n):
        return block_kv.at[buf, i, pl.ds(pl.multiple_of(start, 64), n)]

    def kv_send(k, src, dst, dev):
        return pltpu.make_async_remote_copy(
            src_ref=src, dst_ref=dst, send_sem=ss.at[k], recv_sem=rs.at[k], device_id=dev, device_id_type=MESH
        )

    both = pl.ds(0, 2)
    to_foreign = jnp.where(t == 2, 1, 0)

    def own_to_2(n, i):
        return kv_send(k_own[n], kv_view(0, i, own_start, 128), kv_view(to_foreign, i, own_start, 128), along_z(2))

    def own_to_4(n, i):
        return kv_send(k_own[2 + n], kv_view(0, i, 0, 128), kv_view(1, i, 0, 128), along_z(4))

    def low_to_2():
        return kv_send(k_low, kv_view(0, both, low_start, 64), kv_view(to_foreign, both, low_start, 64), along_z(2))

    def high_to_2():
        return kv_send(
            k_high, kv_view(high_foreign, both, high_start, 64), kv_view(to_foreign, both, high_start, 64), along_z(2)
        )

    def high_to_4():
        return kv_send(
            k_high4, kv_view(high_foreign, both, high_start, 64), kv_view(low_foreign, both, high_start, 64), along_z(4)
        )

    def kv_own(n, i):
        kv = jnp.dot(normed[pl.ds(0, 128)], w_kv[i], preferred_element_type=F32)
        rows = pl.ds(pl.multiple_of(own_start, 128), 128)
        block_kv[0, i, rows, pl.ds(0, 128)] = rope(kv[:, :128], cos_ref[pl.ds(0, 128)], sin_ref[pl.ds(0, 128)]).astype(BF16)
        block_kv[0, i, rows, pl.ds(128, 128)] = kv[:, 128:].astype(BF16)

        @pl.when(t <= 2)
        def _():
            own_to_2(n, i).start()

        @pl.when(t == 0)
        def _():
            own_to_4(n, i).start()

    def kv_near():
        for i in range(2):
            kv = jnp.dot(normed[pl.ds(128, 128)], w_kv[i], preferred_element_type=F32)
            key = rope(kv[:, :128], cos_ref[pl.ds(128, 128)], sin_ref[pl.ds(128, 128)]).astype(BF16)
            value = kv[:, 128:].astype(BF16)
            low_rows = pl.ds(pl.multiple_of(low_start, 64), 64)
            high_rows = pl.ds(pl.multiple_of(high_start, 64), 64)
            block_kv[low_foreign, i, low_rows, pl.ds(0, 128)] = key[:64]
            block_kv[low_foreign, i, low_rows, pl.ds(128, 128)] = value[:64]
            block_kv[high_foreign, i, high_rows, pl.ds(0, 128)] = key[64:]
            block_kv[high_foreign, i, high_rows, pl.ds(128, 128)] = value[64:]
        high_to_2().start()

        @pl.when((t == 1) | (t == 2))
        def _():
            low_to_2().start()

        @pl.when((t == 0) | (t == 3))
        def _():
            high_to_4().start()

    for n in range(4):

        @pl.when(t == n)
        def _(n=n):
            if n < 3:
                start = n * 128 + 192
                block_kv[0, :, pl.ds(start, 512 - start)] = jnp.zeros((2, 512 - start, 256), BF16)
            else:
                block_kv[1, :, pl.ds(64, 448)] = jnp.zeros((2, 448, 256), BF16)

    kv_own(0, slot)

    def q_rows(near, i):
        rows = pl.ds(near * 128, 128)

        @pl.loop(0, 2)
        def _(j):
            c = cos_ref[rows]
            s = sin_ref[rows]
            q = jnp.dot(
                normed[rows], w_q[i, :, :, pl.ds(pl.multiple_of(j * 256, 256), 256)].reshape(4096, 256),
                preferred_element_type=F32,
            )
            for h in range(2):
                v = rope(q[:, h * 128 : (h + 1) * 128], c, s).astype(BF16)
                if near:
                    place = pl.ds(pl.multiple_of((j * 2 + h) * 64, 64), 64)
                    q_near[i, 0, place] = v[:64]
                    q_near[i, 1, place] = v[64:]
                else:
                    q_own[i, j, pl.ds(h * 128, 128)] = v

    q_rows(0, slot)
    q_str.wait_a()
    q_str.first(0)
    q_str.first(1)
    kv_gather.wait_b()

    @pl.when(takes_second)
    def _():
        recv(k_pair, grain, pair)

    @pl.when(takes)
    def _():
        grain_norm[...] = norm(grain[...])

    kv_gather.wait_d()

    k_an = [sem() for _ in range(3)]
    an_mine = an_one(core, b, a)

    def anchor_copy(i):
        return pltpu.make_async_remote_copy(
            src_ref=an_mine, dst_ref=an_mine, send_sem=ss.at[k_an[i]], recv_sem=rs.at[k_an[0]],
            device_id=same_type[i], device_id_type=MESH,
        )

    @pl.when(takes)
    def _():
        c = cos_ref[pl.ds(256, 16)]
        s = sin_ref[pl.ds(256, 16)]
        for i in range(2):
            kv = jnp.dot(grain_norm[...], w_kv[i], preferred_element_type=F32)
            anchor_kv[i, rows16, pl.ds(0, 128)] = rope(kv[:, :128], c, s).astype(BF16)
            anchor_kv[i, rows16, pl.ds(128, 128)] = kv[:, 128:].astype(BF16)
        for i in range(3):
            anchor_copy(i).start()

    kv_own(1, other)
    recv(k_zo, o_str.one(a), wpart)
    o_str.send_a()
    recv(k_norm[0], normed.at[pl.ds(192, 64)], above)
    recv(k_norm[1], normed.at[pl.ds(128, 64)], below)
    kv_near()

    @pl.when(jnp.logical_not(takes))
    def _():
        recv(k_an[0], an_mine, pair)

    an_gather.send_a()
    q_rows(1, slot)
    q_str.on(0)
    q_str.on(1)
    an_gather.wait_a()
    an_gather.send_b()
    o_str.wait_a()
    o_str.first(0)
    o_str.first(1)
    q_str.last(0)
    q_str.last(1)
    an_gather.wait_b()
    q_str.wait_d()
    q_rows(1, other)
    an_gather.wait_d()

    @pl.when(t != 1)
    def _():
        for n in range(2):
            v = kv_view(low_foreign, n, (own_start + 256) % 512, 128)
            kv_send(k_own[n], v, v, along_z(6)).wait_recv()

    @pl.when((t == 0) | (t == 3))
    def _():
        v = kv_view(low_foreign, both, (low_start + 256) % 512, 64)
        kv_send(k_low, v, v, along_z(6)).wait_recv()
        v = kv_view(low_foreign, both, high_start, 64)
        kv_send(k_high4, v, v, along_z(4)).wait_recv()

    @pl.when(t == 0)
    def _():
        for n in range(2):
            v = kv_view(1, n, 0, 128)
            kv_send(k_own[2 + n], v, v, along_z(4)).wait_recv()

    v = kv_view(low_foreign, both, (high_start + 256) % 512, 64)
    recv(k_high, v, along_z(6))

    scale = 1.0 / HD**0.5
    dims = (((1,), (1,)), ((), ()))

    def attend(q, i, buf, block, start, length):
        s1 = lax.dot_general(q, anchor_kv[i, :, pl.ds(0, 128)], dims, preferred_element_type=F32)
        s2 = lax.dot_general(q, block_kv[buf, i, :, pl.ds(0, 128)], dims, preferred_element_type=F32)
        qpos = start + lax.broadcasted_iota(jnp.int32, (256, 512), 0) % length
        kpos = lax.broadcasted_iota(jnp.int32, (256, 512), 1)
        s1 = jnp.where(block == 0, NEG, s1 * scale)
        s2 = jnp.where(kpos <= qpos, s2 * scale, NEG)
        top = jnp.maximum(jnp.max(s1, axis=-1, keepdims=True), jnp.max(s2, axis=-1, keepdims=True))
        e1 = jnp.exp(s1 - top)
        e2 = jnp.exp(s2 - top)
        total = jnp.sum(e1, axis=-1, keepdims=True) + jnp.sum(e2, axis=-1, keepdims=True)
        o = jnp.dot(e1.astype(BF16), anchor_kv[i, :, pl.ds(128, 128)], preferred_element_type=F32)
        o += jnp.dot(e2.astype(BF16), block_kv[buf, i, :, pl.ds(128, 128)], preferred_element_type=F32)
        return (o / total).astype(BF16)

    @pl.loop(0, 2)
    def _(i):
        o = attend(q_near[i, 0], i, low_foreign, low_ctx, low_start, 64)
        for h in range(4):
            att_near[i, pl.ds(0, 64), pl.ds(h * 128, 128)] = o[h * 64 : (h + 1) * 64]
        o = attend(q_near[i, 1], i, high_foreign, high_ctx, high_start, 64)
        for h in range(4):
            att_near[i, pl.ds(64, 64), pl.ds(h * 128, 128)] = o[h * 64 : (h + 1) * 64]

    order = [core * 4 + b, (1 - core) * 4 + a]
    order += [core * 4 + (b + 3) % 4, core * 4 + (b + 1) % 4, (1 - core) * 4 + (a + 3) % 4, (1 - core) * 4 + (a + 1) % 4]
    order += [core * 4 + (b + 2) % 4, (1 - core) * 4 + (a + 2) % 4]
    k_sum = [(sem(), sem()) for _ in range(8)]
    lower, upper = pl.ds(0, 64), pl.ds(64, 64)

    def out_block(att, j):
        return jnp.dot(att[0], w_o[0, j], preferred_element_type=F32) + jnp.dot(att[1], w_o[1, j], preferred_element_type=F32)

    def send_sum(i):
        send_buf[i] = out_block(att_near, order[i]).astype(BF16)
        send(k_sum[i][0], send_buf.at[i, lower], recv_buf.at[i, upper], below)
        send(k_sum[i][1], send_buf.at[i, upper], recv_buf.at[i, lower], above)

    send_sum(0)
    o_str.wait_d((0,))
    send_sum(1)
    o_str.on(0)
    o_str.on(1)
    send_sum(2)
    send_sum(3)
    o_str.wait_d((1, 3))
    send_sum(4)
    send_sum(5)
    o_str.last(0)
    o_str.last(1)
    send_sum(6)
    o_str.wait_d((2,))
    send_sum(7)
    q_rows(0, other)

    @pl.loop(0, 4)
    def _(n):
        i = n // 2
        o = attend(q_own[i, n % 2], i, 0, ctx, own_start, 128)
        for h in range(2):
            att_own[i, :, pl.ds(pl.multiple_of((n % 2) * 256 + h * 128, 128), 128)] = o[h * 128 : (h + 1) * 128]

    @pl.loop(0, 8)
    def _(j):
        cols = pl.ds(pl.multiple_of(j * 512, 512), 512)
        partial[:, cols] = x_ref[:, cols].astype(F32) + out_block(att_own, j)

    @pl.when(is_source)
    def _():
        for j in range(1, 8):
            grain_copy(j).wait_send()

    @pl.when(is_source & (t != 0))
    def _():
        grain_copy(0).wait_send()

    @pl.when(takes_first)
    def _():
        grain_forward().wait_send()

    @pl.when(takes)
    def _():
        for i in range(3):
            anchor_copy(i).wait_send()

    @pl.when(t <= 2)
    def _():
        for n in range(2):
            own_to_2(n, n).wait_send()

    @pl.when(t == 0)
    def _():
        for n in range(2):
            own_to_4(n, n).wait_send()

    high_to_2().wait_send()

    @pl.when((t == 1) | (t == 2))
    def _():
        low_to_2().wait_send()

    @pl.when((t == 0) | (t == 3))
    def _():
        high_to_4().wait_send()

    for cp in sends[:-16]:
        cp.wait_send()
    for i in range(8):
        recv(k_sum[i][0], recv_buf.at[i, upper], above)
        recv(k_sum[i][1], recv_buf.at[i, lower], below)
        cols = pl.ds(pl.multiple_of(order[i] * 512, 512), 512)
        out_ref[:, cols] = (partial[:, cols] + recv_buf[i].astype(F32)).astype(BF16)
    for cp in sends[-16:]:
        cp.wait_send()
    assert count[0] <= N_SEM, count[0]


def angle_tables():
    freq = 500000.0 ** (-(np.arange(HD // 2) * 2.0 / HD))
    sign = np.concatenate([-np.ones(HD // 2), np.ones(HD // 2)])[None]

    def both(positions):
        angle = np.asarray(positions, np.float64)[:, None] * np.concatenate([freq, freq])[None]
        return np.cos(angle).astype(np.float32), (np.sin(angle) * sign).astype(np.float32)

    return (*both(np.arange(128) * 512), *both(np.arange(512)))


def body(hidden_in, norm_gain, w_query, w_key, w_value, w_out, offsets):
    vmem = pl.BlockSpec(memory_space=pltpu.VMEM)
    hbm = pl.BlockSpec(memory_space=pl.ANY)
    return pl.pallas_call(
        kernel,
        out_shape=jax.ShapeDtypeStruct((128, 4096), BF16),
        in_specs=[pl.BlockSpec(memory_space=pltpu.SMEM)] + [vmem] * 6 + [hbm] * 4,
        out_specs=vmem,
        scratch_shapes=[
            pltpu.VMEM((2, 8, 512, 512), BF16),
            pltpu.VMEM((2, 4096, 256), BF16),
            pltpu.VMEM((2, 8, 512, 512), BF16),
            pltpu.VMEM((256, 4096), BF16),
            pltpu.VMEM((16, 4096), BF16),
            pltpu.VMEM((16, 4096), BF16),
            pltpu.VMEM((2, 512, 256), BF16),
            pltpu.VMEM((2, 2, 512, 256), BF16),
            pltpu.VMEM((2, 2, 256, 128), BF16),
            pltpu.VMEM((2, 2, 256, 128), BF16),
            pltpu.VMEM((2, 128, 512), BF16),
            pltpu.VMEM((2, 128, 512), BF16),
            pltpu.VMEM((8, 128, 512), BF16),
            pltpu.VMEM((8, 128, 512), BF16),
            pltpu.VMEM((128, 4096), F32),
            pltpu.VMEM((272, 128), F32),
            pltpu.VMEM((272, 128), F32),
            pltpu.SemaphoreType.DMA((N_SEM,)),
            pltpu.SemaphoreType.DMA((N_SEM,)),
            pltpu.SemaphoreType.DMA((19,)),
        ],
        compiler_params=pltpu.CompilerParams(collective_id=0, has_side_effects=True, vmem_limit_bytes=56 * 2**20),
        cost_estimate=pl.CostEstimate(flops=10**10, bytes_accessed=2 * 10**7, transcendentals=2 * 10**6),
    )(offsets, hidden_in, norm_gain.reshape(1, 4096), *angle_tables(), w_query, w_key, w_value, w_out)


def solution(mesh):
    placed = (
        P(("context", "tensor"), None),
        P(),
        P(None, "tensor"),
        P(None, "tensor"),
        P(None, "tensor"),
        P("tensor", None),
        P(),
    )
    return jax.shard_map(
        body, mesh=mesh, in_specs=placed, out_specs=P(("context", "tensor"), None), check_vma=False
    )
```

```python
import jax
import jax.numpy as jnp
import numpy as np
from jax import lax
from jax.experimental import pallas as pl
from jax.experimental.pallas import tpu as pltpu
from jax.sharding import PartitionSpec as P

HD = 128
EPS = 1e-05
NEG = -1e30
MESH = pl.DeviceIdType.MESH
F32 = jnp.float32
BF16 = jnp.bfloat16
N_SEM = 144


def kernel(
    offsets_ref, gain_ref, x_hbm, tables_hbm, wq_hbm, wk_hbm, wv_hbm, wo_hbm, out_ref,
    w_q, w_kv, w_o, normed, grain, grain_norm, anchor_kv, block_kv, q_own, q_near, att_own, att_near, send_buf, recv_buf,
    partial, cos_ref, sin_ref, x_ref, tables_ref, ss, rs, ls,
):
    ctx = lax.axis_index("context")
    t = lax.axis_index("tensor")
    core = ctx % 2
    y = (ctx // 2) % 4
    zh = (ctx // 8) % 2
    x = ctx // 16
    a = x * (1 - core) + y * core
    b = y * (1 - core) + x * core
    m = b * 4 + a
    mine = core * 16 + m
    slot = t // 2
    other = 1 - slot
    parity = t % 2

    def at(x_, y_, zh_, t_, core_):
        return (((x_ * 2 + zh_) * 4 + y_) * 2 + core_, t_)

    def ring_a(d):
        return at((x + d * (1 - core)) % 4, (y + d * core) % 4, zh, t, core)

    def ring_b(d):
        return at((x + d * core) % 4, (y + d * (1 - core)) % 4, zh, t, core)

    def along_z(d):
        z = (zh * 4 + t + d) % 8
        return at(x, y, z // 4, z % 4, core)

    sibling = at(x, y, zh, t, 1 - core)
    above, below = along_z(1), along_z(7)
    pair = at(x, y, zh, t + 1 - 2 * parity, core)
    wpart = at(x, y, (zh + core) % 2, (t + 2) % 4, core)
    same_type = [along_z(2), along_z(4), along_z(6)]
    foreign = ctx + 8 - 16 * zh
    low_foreign = jnp.where(t == 0, 1, 0)
    high_foreign = jnp.where(t == 3, 1, 0)
    low_ctx = ctx + (foreign - ctx) * low_foreign
    high_ctx = ctx + (foreign - ctx) * high_foreign
    own_start = t * 128
    low_start = (t * 128 + 448) % 512
    high_start = (t * 128 + 128) % 512

    count = [0]
    sends = []

    def sem():
        count[0] += 1
        return count[0] - 1

    def send(k, src, dst, dev, keep=True):
        cp = pltpu.make_async_remote_copy(
            src_ref=src, dst_ref=dst, send_sem=ss.at[k], recv_sem=rs.at[k], device_id=dev, device_id_type=MESH
        )
        cp.start()
        if keep:
            sends.append(cp)
        return cp

    def recv(k, dst, dev):
        pltpu.make_async_remote_copy(
            src_ref=dst, dst_ref=dst, send_sem=ss.at[k], recv_sem=rs.at[k], device_id=dev, device_id_type=MESH
        ).wait_recv()

    is_source = ctx == 0
    takes = (zh == 0) & (core == slot)
    takes_first = takes & (m // 8 == parity)
    takes_second = takes & (m // 8 != parity)
    self_grain = is_source & (t == 0)

    bar = pltpu.get_barrier_semaphore()
    peers = [ring_a(d) for d in (1, 2, 3)] + [ring_b(d) for d in (1, 2, 3)] + [sibling, above, below] + same_type
    for d in (1, 2, 3):
        for dz in (2, 4, 6):
            z = (zh * 4 + t + dz) % 8
            peers.append(at((x + d * (1 - core)) % 4, (y + d * core) % 4, z // 4, z % 4, core))
    for p in peers:
        pl.semaphore_signal(bar, inc=1, device_id=p, device_id_type=MESH)

    @pl.when(takes_first & jnp.logical_not(self_grain))
    def _():
        pl.semaphore_signal(bar, inc=1, device_id=(0, t), device_id_type=MESH)

    x_load = pltpu.make_async_copy(x_hbm, x_ref, ls.at[19])
    x_load.start()
    table_load = pltpu.make_async_copy(tables_hbm, tables_ref, ls.at[20])
    table_load.start()
    loads = []
    for i, (src, dst) in enumerate(
        [
            (wk_hbm, w_kv.at[slot, :, pl.ds(0, 128)]),
            (wv_hbm, w_kv.at[slot, :, pl.ds(128, 128)]),
        ]
        + [(wq_hbm.at[pl.ds(j * 512, 512)], w_q.at[slot, j]) for j in range(8)]
        + [(wo_hbm.at[:, pl.ds(j * 512, 512)], w_o.at[slot, j]) for j in range(8)]
    ):
        cp = pltpu.make_async_copy(src, dst, ls.at[i])
        cp.start()
        loads.append(cp)

    def fill_tables(at_row, n, row, offset):
        cb = tables_ref[0, pl.ds(512 + offset, 1)]
        sb = tables_ref[1, pl.ds(512 + offset, 1)]
        cr = tables_ref[0, pl.ds(row, n)]
        sr = tables_ref[1, pl.ds(row, n)]
        cos_ref[pl.ds(at_row, n)] = cb * cr - sb * sr
        sin_ref[pl.ds(at_row, n)] = sb * cr + cb * sr

    grains_out = jnp.where(is_source, jnp.where(t == 0, 7, 8), 0)
    pl.semaphore_wait(bar, len(peers) + grains_out)

    rows128 = pl.ds(pl.multiple_of(mine * 128, 128), 128)
    rows16 = pl.ds(pl.multiple_of(mine * 16, 16), 16)
    my_block = core * 4 + b
    o_cols = pl.ds(pl.multiple_of(my_block * 512, 512), 512)
    quarter = pl.ds(pl.multiple_of(a * 128, 128), 128)
    k_zk, k_zv, k_zq, k_zo = sem(), sem(), sem(), sem()
    send(k_zk, wk_hbm.at[rows128], w_kv.at[slot, rows128, pl.ds(0, 128)], wpart)
    send(k_zv, wv_hbm.at[rows128], w_kv.at[slot, rows128, pl.ds(128, 128)], wpart)
    send(k_zq, wq_hbm.at[rows128], w_q.at[slot, my_block, quarter], wpart)
    send(k_zo, wo_hbm.at[quarter, o_cols], w_o.at[slot, my_block, quarter], wpart)

    x_load.wait()
    k_scat = [sem() for _ in range(8)]

    def grain_target(j):
        mm = 8 * parity + j
        aa = mm % 4
        bb = mm // 4
        return at(aa * (1 - slot) + bb * slot, bb * (1 - slot) + aa * slot, 0, t, slot)

    def grain_copy(j):
        return pltpu.make_async_remote_copy(
            src_ref=x_ref.at[pl.ds(16 * j, 16)], dst_ref=grain, send_sem=ss.at[k_scat[j]], recv_sem=rs.at[k_scat[0]],
            device_id=grain_target(j), device_id_type=MESH,
        )

    @pl.when(is_source)
    def _():
        for j in range(1, 8):
            grain_copy(j).start()

    @pl.when(is_source & (t != 0))
    def _():
        grain_copy(0).start()

    @pl.when(self_grain)
    def _():
        cp = pltpu.make_async_copy(x_ref.at[pl.ds(0, 16)], grain, ls.at[18])
        cp.start()
        cp.wait()

    def kv_one(c_, b_, a_):
        return w_kv.at[other, pl.ds(pl.multiple_of((c_ * 16 + b_ * 4 + a_) * 128, 128), 128)]

    def kv_block(c_, b_):
        return w_kv.at[other, pl.ds(pl.multiple_of((c_ * 4 + b_) * 512, 512), 512)]

    def an_one(c_, b_, a_):
        return anchor_kv.at[:, pl.ds(pl.multiple_of((c_ * 16 + b_ * 4 + a_) * 16, 16), 16)]

    def an_block(c_, b_):
        return anchor_kv.at[:, pl.ds(pl.multiple_of((c_ * 4 + b_) * 64, 64), 64)]

    class Gather:
        def __init__(self, one, block):
            self.one, self.block = one, block
            self.ka = [sem() for _ in range(3)] if one else []
            self.kb = [sem() for _ in range(3)]
            self.kd = [sem() for _ in range(4)]

        def send_a(self):
            v = self.one(core, b, a)
            for d in (1, 3, 2):
                send(self.ka[d - 1], v, v, ring_a(d))

        def wait_a(self):
            for d in (1, 3, 2):
                recv(self.ka[d - 1], self.one(core, b, (a + 4 - d) % 4), ring_a(4 - d))

        def send_b(self):
            v = self.block(core, b)
            for d in (1, 3, 2):
                send(self.kb[d - 1], v, v, ring_b(d))
            send(self.kd[0], v, v, sibling)

        def wait_b(self):
            for d in (1, 3, 2):
                v = self.block(core, (b + 4 - d) % 4)
                recv(self.kb[d - 1], v, ring_b(4 - d))
                send(self.kd[d], v, v, sibling)

        def wait_d(self):
            for d in (0, 1, 3, 2):
                recv(self.kd[d], self.block(1 - core, (a + 4 - d) % 4), sibling)

    class Stream:
        def __init__(self, block, pieces, slices):
            self.block, self.n, self.g = block, pieces, 512 // pieces
            self.ka = [sem() for _ in range(3)] if slices else []
            self.kb = [[sem() for _ in range(2)] for _ in range(pieces)]
            self.kc = [[sem() for _ in range(2)] for _ in range(pieces)]
            self.kd = [[sem() for _ in range(4)] for _ in range(pieces)]

        def piece(self, c_, b_, k):
            return self.block(c_, b_, pl.ds(k * self.g, self.g))

        def half(self, b_, k, h):
            return self.block(core, b_, pl.ds(k * self.g + h * (self.g // 2), self.g // 2))

        def one(self, a_):
            return self.block(core, b, pl.ds(pl.multiple_of(a_ * 128, 128), 128))

        def send_a(self):
            v = self.one(a)
            for d in (1, 3, 2):
                send(self.ka[d - 1], v, v, ring_a(d))

        def wait_a(self):
            for d in (1, 3, 2):
                recv(self.ka[d - 1], self.one((a + 4 - d) % 4), ring_a(4 - d))

        def first(self, k):
            v = self.piece(core, b, k)
            for i, d in enumerate((1, 3)):
                send(self.kb[k][i], v, v, ring_b(d))
            send(self.kd[k][0], v, v, sibling)

        def on(self, k):
            for i, d in enumerate((1, 3)):
                near = (b + 4 - d) % 4
                recv(self.kb[k][i], self.piece(core, near, k), ring_b(4 - d))
                v = self.half(near, k, i)
                send(self.kc[k][i], v, v, ring_b(d))
                v = self.piece(core, near, k)
                send(self.kd[k][d], v, v, sibling)

        def last(self, k):
            far_b = (b + 2) % 4
            for i, d in enumerate((1, 3)):
                recv(self.kc[k][i], self.half(far_b, k, i), ring_b(4 - d))
            v = self.piece(core, far_b, k)
            send(self.kd[k][2], v, v, sibling)

        def wait_d(self, ds=(0, 1, 3, 2)):
            for d in ds:
                for k in range(self.n):
                    recv(self.kd[k][d], self.piece(1 - core, (a + 4 - d) % 4, k), sibling)

    def q_view(c_, b_, rows):
        return w_q.at[other, c_ * 4 + b_, rows]

    def o_view(c_, b_, rows):
        return w_o.at[other, c_ * 4 + b_, rows]

    kv_gather = Gather(kv_one, kv_block)
    an_gather = Gather(None, an_block)
    q_str = Stream(q_view, 4, True)
    o_str = Stream(o_view, 2, True)

    def norm(rows):
        v = rows.astype(F32)
        mean_sq = jnp.mean(v * v, axis=-1, keepdims=True)
        return (v * lax.rsqrt(mean_sq + EPS) * gain_ref[...]).astype(BF16)

    k_norm = [sem() for _ in range(4)]
    for i in range(2):

        @pl.loop(0, 4)
        def _(r, i=i):
            rr = pl.ds(pl.multiple_of(i * 64 + r * 16, 16), 16)
            normed[rr] = norm(x_ref[rr])

        if i == 0:
            send(k_norm[0], normed.at[pl.ds(0, 32)], normed.at[pl.ds(192, 32)], below)
        else:
            send(k_norm[1], normed.at[pl.ds(64, 32)], normed.at[pl.ds(128, 32)], above)

    recv(k_zk, w_kv.at[other, rows128, pl.ds(0, 128)], wpart)
    recv(k_zv, w_kv.at[other, rows128, pl.ds(128, 128)], wpart)
    kv_gather.send_a()

    k_pair = sem()

    def grain_forward():
        return pltpu.make_async_remote_copy(
            src_ref=grain, dst_ref=grain, send_sem=ss.at[k_pair], recv_sem=rs.at[k_pair], device_id=pair, device_id_type=MESH
        )

    @pl.when(takes_first & jnp.logical_not(self_grain))
    def _():
        recv(k_scat[0], grain, (0, t))

    @pl.when(takes_first)
    def _():
        grain_forward().start()

    send(k_norm[2], normed.at[pl.ds(32, 32)], normed.at[pl.ds(224, 32)], below)
    send(k_norm[3], normed.at[pl.ds(96, 32)], normed.at[pl.ds(160, 32)], above)

    recv(k_zq, q_str.one(a), wpart)
    q_str.send_a()
    kv_gather.wait_a()
    kv_gather.send_b()
    recv(k_zo, o_str.one(a), wpart)
    o_str.send_a()
    table_load.wait()
    fill_tables(0, 128, pl.multiple_of(own_start, 128), offsets_ref[ctx])
    fill_tables(128, 64, pl.multiple_of(low_start, 64), offsets_ref[low_ctx])
    fill_tables(192, 64, pl.multiple_of(high_start, 64), offsets_ref[high_ctx])
    fill_tables(256, 16, pl.multiple_of(mine * 16, 16), offsets_ref[0])
    for cp in loads:
        cp.wait()

    def rope(v, c, s):
        return v * c + pltpu.roll(v, 64, 1) * s

    k_own = [sem() for _ in range(4)]
    k_low, k_high, k_high4 = sem(), sem(), sem()

    def kv_view(buf, i, start, n):
        return block_kv.at[buf, i, pl.ds(pl.multiple_of(start, 64), n)]

    def kv_send(k, src, dst, dev):
        return pltpu.make_async_remote_copy(
            src_ref=src, dst_ref=dst, send_sem=ss.at[k], recv_sem=rs.at[k], device_id=dev, device_id_type=MESH
        )

    both = pl.ds(0, 2)
    to_foreign = jnp.where(t == 2, 1, 0)

    def own_to_2(n, i):
        return kv_send(k_own[n], kv_view(0, i, own_start, 128), kv_view(to_foreign, i, own_start, 128), along_z(2))

    def own_to_4(n, i):
        return kv_send(k_own[2 + n], kv_view(0, i, 0, 128), kv_view(1, i, 0, 128), along_z(4))

    def low_to_2():
        return kv_send(k_low, kv_view(0, both, low_start, 64), kv_view(to_foreign, both, low_start, 64), along_z(2))

    def high_to_2():
        return kv_send(
            k_high, kv_view(high_foreign, both, high_start, 64), kv_view(to_foreign, both, high_start, 64), along_z(2)
        )

    def high_to_4():
        return kv_send(
            k_high4, kv_view(high_foreign, both, high_start, 64), kv_view(low_foreign, both, high_start, 64), along_z(4)
        )

    def kv_own(n, i):
        kv = jnp.dot(normed[pl.ds(0, 128)], w_kv[i], preferred_element_type=F32)
        rows = pl.ds(pl.multiple_of(own_start, 128), 128)
        block_kv[0, i, rows, pl.ds(0, 128)] = rope(kv[:, :128], cos_ref[pl.ds(0, 128)], sin_ref[pl.ds(0, 128)]).astype(BF16)
        block_kv[0, i, rows, pl.ds(128, 128)] = kv[:, 128:].astype(BF16)

        @pl.when(t <= 2)
        def _():
            own_to_2(n, i).start()

        @pl.when(t == 0)
        def _():
            own_to_4(n, i).start()

    def kv_near():
        for i in range(2):
            kv = jnp.dot(normed[pl.ds(128, 128)], w_kv[i], preferred_element_type=F32)
            key = rope(kv[:, :128], cos_ref[pl.ds(128, 128)], sin_ref[pl.ds(128, 128)]).astype(BF16)
            value = kv[:, 128:].astype(BF16)
            low_rows = pl.ds(pl.multiple_of(low_start, 64), 64)
            high_rows = pl.ds(pl.multiple_of(high_start, 64), 64)
            block_kv[low_foreign, i, low_rows, pl.ds(0, 128)] = key[:64]
            block_kv[low_foreign, i, low_rows, pl.ds(128, 128)] = value[:64]
            block_kv[high_foreign, i, high_rows, pl.ds(0, 128)] = key[64:]
            block_kv[high_foreign, i, high_rows, pl.ds(128, 128)] = value[64:]
        high_to_2().start()

        @pl.when((t == 1) | (t == 2))
        def _():
            low_to_2().start()

        @pl.when((t == 0) | (t == 3))
        def _():
            high_to_4().start()

    for n in range(4):

        @pl.when(t == n)
        def _(n=n):
            if n < 3:
                start = n * 128 + 192
                block_kv[0, :, pl.ds(start, 512 - start)] = jnp.zeros((2, 512 - start, 256), BF16)
            else:
                block_kv[1, :, pl.ds(64, 448)] = jnp.zeros((2, 448, 256), BF16)

    kv_own(0, slot)

    def q_rows(near, i):
        rows = pl.ds(near * 128, 128)

        @pl.loop(0, 2)
        def _(j):
            c = cos_ref[rows]
            s = sin_ref[rows]
            q = jnp.dot(
                normed[rows], w_q[i, :, :, pl.ds(pl.multiple_of(j * 256, 256), 256)].reshape(4096, 256),
                preferred_element_type=F32,
            )
            for h in range(2):
                v = rope(q[:, h * 128 : (h + 1) * 128], c, s).astype(BF16)
                if near:
                    place = pl.ds(pl.multiple_of((j * 2 + h) * 64, 64), 64)
                    q_near[i, 0, place] = v[:64]
                    q_near[i, 1, place] = v[64:]
                else:
                    q_own[i, j, pl.ds(h * 128, 128)] = v

    q_rows(0, slot)
    q_str.wait_a()
    q_str.first(0)
    q_str.first(1)
    q_str.first(2)
    q_str.first(3)
    kv_gather.wait_b()

    @pl.when(takes_second)
    def _():
        recv(k_pair, grain, pair)

    @pl.when(takes)
    def _():
        grain_norm[...] = norm(grain[...])

    kv_gather.wait_d()

    k_an = [sem() for _ in range(15)]
    k_an_in = [sem() for _ in range(4)]
    an_mine = an_one(core, b, a)
    zs, ds = (0, 2, 4, 6), (0, 1, 3, 2)

    def anchor_copy(n):
        dz, d = [(i, j) for j in ds for i in zs][1:][n]
        z = (zh * 4 + t + dz) % 8
        dev = at((x + d * (1 - core)) % 4, (y + d * core) % 4, z // 4, z % 4, core)
        return pltpu.make_async_remote_copy(
            src_ref=an_mine, dst_ref=an_mine, send_sem=ss.at[k_an[n]], recv_sem=rs.at[k_an_in[d]],
            device_id=dev, device_id_type=MESH,
        )

    @pl.when(takes)
    def _():
        c = cos_ref[pl.ds(256, 16)]
        s = sin_ref[pl.ds(256, 16)]
        for i in range(2):
            kv = jnp.dot(grain_norm[...], w_kv[i], preferred_element_type=F32)
            anchor_kv[i, rows16, pl.ds(0, 128)] = rope(kv[:, :128], c, s).astype(BF16)
            anchor_kv[i, rows16, pl.ds(128, 128)] = kv[:, 128:].astype(BF16)
        for i in range(15):
            anchor_copy(i).start()

    kv_own(1, other)
    q_str.on(0)
    q_str.on(1)
    recv(k_norm[0], normed.at[pl.ds(192, 32)], above)
    recv(k_norm[1], normed.at[pl.ds(128, 32)], below)
    recv(k_norm[2], normed.at[pl.ds(224, 32)], above)
    recv(k_norm[3], normed.at[pl.ds(160, 32)], below)
    kv_near()

    q_str.on(2)
    q_str.on(3)
    o_str.wait_a()
    o_str.first(0)
    o_str.first(1)
    q_rows(1, slot)

    @pl.when(jnp.logical_not(takes))
    def _():
        recv(k_an_in[0], an_mine, pair)

    for d in (1, 3, 2):
        recv(k_an_in[d], an_one(core, b, (a + 4 - d) % 4), pair)
    an_gather.send_b()
    q_str.last(0)
    q_str.last(1)
    q_str.last(2)
    q_str.last(3)
    an_gather.wait_b()
    q_str.wait_d()
    o_str.on(0)
    q_rows(1, other)
    o_str.on(1)
    an_gather.wait_d()

    @pl.when(t != 1)
    def _():
        for n in range(2):
            v = kv_view(low_foreign, n, (own_start + 256) % 512, 128)
            kv_send(k_own[n], v, v, along_z(6)).wait_recv()

    @pl.when((t == 0) | (t == 3))
    def _():
        v = kv_view(low_foreign, both, (low_start + 256) % 512, 64)
        kv_send(k_low, v, v, along_z(6)).wait_recv()
        v = kv_view(low_foreign, both, high_start, 64)
        kv_send(k_high4, v, v, along_z(4)).wait_recv()

    @pl.when(t == 0)
    def _():
        for n in range(2):
            v = kv_view(1, n, 0, 128)
            kv_send(k_own[2 + n], v, v, along_z(4)).wait_recv()

    v = kv_view(low_foreign, both, (high_start + 256) % 512, 64)
    recv(k_high, v, along_z(6))

    scale = 1.0 / HD**0.5
    dims = (((1,), (1,)), ((), ()))

    def attend(q, i, buf, block, start, length):
        s1 = lax.dot_general(q, anchor_kv[i, :, pl.ds(0, 128)], dims, preferred_element_type=F32)
        s2 = lax.dot_general(q, block_kv[buf, i, :, pl.ds(0, 128)], dims, preferred_element_type=F32)
        qpos = start + lax.broadcasted_iota(jnp.int32, (256, 512), 0) % length
        kpos = lax.broadcasted_iota(jnp.int32, (256, 512), 1)
        s1 = jnp.where(block == 0, NEG, s1 * scale)
        s2 = jnp.where(kpos <= qpos, s2 * scale, NEG)
        top = jnp.maximum(jnp.max(s1, axis=-1, keepdims=True), jnp.max(s2, axis=-1, keepdims=True))
        e1 = jnp.exp(s1 - top)
        e2 = jnp.exp(s2 - top)
        total = jnp.sum(e1, axis=-1, keepdims=True) + jnp.sum(e2, axis=-1, keepdims=True)
        o = jnp.dot(e1.astype(BF16), anchor_kv[i, :, pl.ds(128, 128)], preferred_element_type=F32)
        o += jnp.dot(e2.astype(BF16), block_kv[buf, i, :, pl.ds(128, 128)], preferred_element_type=F32)
        return (o / total).astype(BF16)

    @pl.loop(0, 2)
    def _(i):
        o = attend(q_near[i, 0], i, low_foreign, low_ctx, low_start, 64)
        for h in range(4):
            att_near[i, pl.ds(0, 64), pl.ds(h * 128, 128)] = o[h * 64 : (h + 1) * 64]
        o = attend(q_near[i, 1], i, high_foreign, high_ctx, high_start, 64)
        for h in range(4):
            att_near[i, pl.ds(64, 64), pl.ds(h * 128, 128)] = o[h * 64 : (h + 1) * 64]

    order = [core * 4 + b, (1 - core) * 4 + a]
    order += [core * 4 + (b + 3) % 4, core * 4 + (b + 1) % 4, (1 - core) * 4 + (a + 3) % 4, (1 - core) * 4 + (a + 1) % 4]
    order += [core * 4 + (b + 2) % 4, (1 - core) * 4 + (a + 2) % 4]
    k_sum = [(sem(), sem()) for _ in range(8)]
    lower, upper = pl.ds(0, 64), pl.ds(64, 64)

    def out_block(att, j):
        return jnp.dot(att[0], w_o[0, j], preferred_element_type=F32) + jnp.dot(att[1], w_o[1, j], preferred_element_type=F32)

    def send_sum(i):
        send_buf[i] = out_block(att_near, order[i]).astype(BF16)
        send(k_sum[i][0], send_buf.at[i, lower], recv_buf.at[i, upper], below)
        send(k_sum[i][1], send_buf.at[i, upper], recv_buf.at[i, lower], above)

    send_sum(0)
    o_str.wait_d((0,))
    send_sum(1)
    send_sum(2)
    send_sum(3)
    o_str.wait_d((1, 3))
    send_sum(4)
    send_sum(5)
    o_str.last(0)
    o_str.last(1)
    send_sum(6)
    o_str.wait_d((2,))
    send_sum(7)
    q_rows(0, other)

    @pl.loop(0, 4)
    def _(n):
        i = n // 2
        o = attend(q_own[i, n % 2], i, 0, ctx, own_start, 128)
        for h in range(2):
            att_own[i, :, pl.ds(pl.multiple_of((n % 2) * 256 + h * 128, 128), 128)] = o[h * 128 : (h + 1) * 128]

    @pl.loop(0, 8)
    def _(j):
        cols = pl.ds(pl.multiple_of(j * 512, 512), 512)
        partial[:, cols] = x_ref[:, cols].astype(F32) + out_block(att_own, j)

    @pl.when(is_source)
    def _():
        for j in range(1, 8):
            grain_copy(j).wait_send()

    @pl.when(is_source & (t != 0))
    def _():
        grain_copy(0).wait_send()

    @pl.when(takes_first)
    def _():
        grain_forward().wait_send()

    @pl.when(takes)
    def _():
        for i in range(15):
            anchor_copy(i).wait_send()

    @pl.when(t <= 2)
    def _():
        for n in range(2):
            own_to_2(n, n).wait_send()

    @pl.when(t == 0)
    def _():
        for n in range(2):
            own_to_4(n, n).wait_send()

    high_to_2().wait_send()

    @pl.when((t == 1) | (t == 2))
    def _():
        low_to_2().wait_send()

    @pl.when((t == 0) | (t == 3))
    def _():
        high_to_4().wait_send()

    for cp in sends[:-16]:
        cp.wait_send()
    for i in range(8):
        recv(k_sum[i][0], recv_buf.at[i, upper], above)
        recv(k_sum[i][1], recv_buf.at[i, lower], below)
        cols = pl.ds(pl.multiple_of(order[i] * 512, 512), 512)
        out_ref[:, cols] = (partial[:, cols] + recv_buf[i].astype(F32)).astype(BF16)
    for cp in sends[-16:]:
        cp.wait_send()
    assert count[0] <= N_SEM, count[0]


def angle_tables():
    freq = 500000.0 ** (-(np.arange(HD // 2) * 2.0 / HD))
    sign = np.concatenate([-np.ones(HD // 2), np.ones(HD // 2)])[None]

    def both(positions):
        angle = np.asarray(positions, np.float64)[:, None] * np.concatenate([freq, freq])[None]
        return np.cos(angle).astype(np.float32), (np.sin(angle) * sign).astype(np.float32)

    return np.stack(both(np.concatenate([np.arange(512), np.arange(128) * 512])))


def body(hidden_in, norm_gain, w_query, w_key, w_value, w_out, offsets):
    vmem = pl.BlockSpec(memory_space=pltpu.VMEM)
    hbm = pl.BlockSpec(memory_space=pl.ANY)
    return pl.pallas_call(
        kernel,
        out_shape=jax.ShapeDtypeStruct((128, 4096), BF16),
        in_specs=[pl.BlockSpec(memory_space=pltpu.SMEM), vmem] + [hbm] * 6,
        out_specs=vmem,
        scratch_shapes=[
            pltpu.VMEM((2, 8, 512, 512), BF16),
            pltpu.VMEM((2, 4096, 256), BF16),
            pltpu.VMEM((2, 8, 512, 512), BF16),
            pltpu.VMEM((256, 4096), BF16),
            pltpu.VMEM((16, 4096), BF16),
            pltpu.VMEM((16, 4096), BF16),
            pltpu.VMEM((2, 512, 256), BF16),
            pltpu.VMEM((2, 2, 512, 256), BF16),
            pltpu.VMEM((2, 2, 256, 128), BF16),
            pltpu.VMEM((2, 2, 256, 128), BF16),
            pltpu.VMEM((2, 128, 512), BF16),
            pltpu.VMEM((2, 128, 512), BF16),
            pltpu.VMEM((8, 128, 512), BF16),
            pltpu.VMEM((8, 128, 512), BF16),
            pltpu.VMEM((128, 4096), F32),
            pltpu.VMEM((272, 128), F32),
            pltpu.VMEM((272, 128), F32),
            pltpu.VMEM((128, 4096), BF16),
            pltpu.VMEM((2, 640, 128), F32),
            pltpu.SemaphoreType.DMA((N_SEM,)),
            pltpu.SemaphoreType.DMA((N_SEM,)),
            pltpu.SemaphoreType.DMA((21,)),
        ],
        compiler_params=pltpu.CompilerParams(collective_id=0, has_side_effects=True, vmem_limit_bytes=56 * 2**20),
        cost_estimate=pl.CostEstimate(flops=10**10, bytes_accessed=2 * 10**7, transcendentals=2 * 10**6),
    )(offsets, norm_gain.reshape(1, 4096), hidden_in, angle_tables(), w_query, w_key, w_value, w_out)


def solution(mesh):
    placed = (
        P(("context", "tensor"), None),
        P(),
        P(None, "tensor"),
        P(None, "tensor"),
        P(None, "tensor"),
        P("tensor", None),
        P(),
    )
    return jax.shard_map(
        body, mesh=mesh, in_specs=placed, out_specs=P(("context", "tensor"), None), check_vma=False
    )
```

```python
import jax
import jax.numpy as jnp
import numpy as np
from jax import lax
from jax.experimental import pallas as pl
from jax.experimental.pallas import tpu as pltpu
from jax.sharding import PartitionSpec as P

HD = 128
EPS = 1e-05
NEG = -1e30
LOG2_E = 1.4426950408889634
MESH = pl.DeviceIdType.MESH
F32 = jnp.float32
BF16 = jnp.bfloat16
N_SEM = 144


def kernel(
    offsets_ref, gain_ref, x_hbm, tables_hbm, wq_hbm, wk_hbm, wv_hbm, wo_hbm, out_ref,
    w_q, w_kv, w_o, normed, grain, grain_norm, anchor_kv, block_kv, q_own, q_near, att_own, att_near, send_buf, recv_buf,
    partial, cos_ref, sin_ref, x_ref, tables_ref, out_buf, ss, rs, ls,
):
    ctx = lax.axis_index("context")
    t = lax.axis_index("tensor")
    core = ctx % 2
    y = (ctx // 2) % 4
    zh = (ctx // 8) % 2
    x = ctx // 16
    a = x * (1 - core) + y * core
    b = y * (1 - core) + x * core
    m = b * 4 + a
    mine = core * 16 + m
    slot = t // 2
    other = 1 - slot
    parity = t % 2

    def at(x_, y_, zh_, t_, core_):
        return (((x_ * 2 + zh_) * 4 + y_) * 2 + core_, t_)

    def ring_a(d):
        return at((x + d * (1 - core)) % 4, (y + d * core) % 4, zh, t, core)

    def ring_b(d):
        return at((x + d * core) % 4, (y + d * (1 - core)) % 4, zh, t, core)

    def along_z(d):
        z = (zh * 4 + t + d) % 8
        return at(x, y, z // 4, z % 4, core)

    sibling = at(x, y, zh, t, 1 - core)
    above, below = along_z(1), along_z(7)
    pair = at(x, y, zh, t + 1 - 2 * parity, core)
    wpart = at(x, y, (zh + core) % 2, (t + 2) % 4, core)
    same_type = [along_z(2), along_z(4), along_z(6)]
    foreign = ctx + 8 - 16 * zh
    low_foreign = jnp.where(t == 0, 1, 0)
    high_foreign = jnp.where(t == 3, 1, 0)
    low_ctx = ctx + (foreign - ctx) * low_foreign
    high_ctx = ctx + (foreign - ctx) * high_foreign
    own_start = t * 128
    low_start = (t * 128 + 448) % 512
    high_start = (t * 128 + 128) % 512

    count = [0]
    sends = []

    def sem():
        count[0] += 1
        return count[0] - 1

    def send(k, src, dst, dev, keep=True):
        cp = pltpu.make_async_remote_copy(
            src_ref=src, dst_ref=dst, send_sem=ss.at[k], recv_sem=rs.at[k], device_id=dev, device_id_type=MESH
        )
        cp.start()
        if keep:
            sends.append(cp)
        return cp

    def recv(k, dst, dev):
        pltpu.make_async_remote_copy(
            src_ref=dst, dst_ref=dst, send_sem=ss.at[k], recv_sem=rs.at[k], device_id=dev, device_id_type=MESH
        ).wait_recv()

    is_source = ctx == 0
    takes = (zh == 0) & (core == slot)
    takes_first = takes & (m // 8 == parity)
    takes_second = takes & (m // 8 != parity)
    self_grain = is_source & (t == 0)

    bar = pltpu.get_barrier_semaphore()
    peers = [ring_a(d) for d in (1, 2, 3)] + [ring_b(d) for d in (1, 2, 3)] + [sibling, above, below] + same_type
    for d in (1, 2, 3):
        for dz in (2, 4, 6):
            z = (zh * 4 + t + dz) % 8
            peers.append(at((x + d * (1 - core)) % 4, (y + d * core) % 4, z // 4, z % 4, core))
    for p in peers:
        pl.semaphore_signal(bar, inc=1, device_id=p, device_id_type=MESH)

    @pl.when(takes_first & jnp.logical_not(self_grain))
    def _():
        pl.semaphore_signal(bar, inc=1, device_id=(0, t), device_id_type=MESH)

    x_load = pltpu.make_async_copy(x_hbm, x_ref, ls.at[19])
    x_load.start()
    table_load = pltpu.make_async_copy(tables_hbm, tables_ref, ls.at[20])
    table_load.start()
    loads = []
    for i, (src, dst) in enumerate(
        [
            (wk_hbm, w_kv.at[slot, :, pl.ds(0, 128)]),
            (wv_hbm, w_kv.at[slot, :, pl.ds(128, 128)]),
        ]
        + [(wq_hbm.at[pl.ds(j * 512, 512)], w_q.at[slot, j]) for j in range(8)]
        + [(wo_hbm.at[:, pl.ds(j * 512, 512)], w_o.at[slot, j]) for j in range(8)]
    ):
        cp = pltpu.make_async_copy(src, dst, ls.at[i])
        cp.start()
        loads.append(cp)

    def fill_tables(at_row, n, row, offset):
        cb = tables_ref[0, pl.ds(512 + offset, 1)]
        sb = tables_ref[1, pl.ds(512 + offset, 1)]
        cr = tables_ref[0, pl.ds(row, n)]
        sr = tables_ref[1, pl.ds(row, n)]
        cos_ref[pl.ds(at_row, n)] = cb * cr - sb * sr
        sin_ref[pl.ds(at_row, n)] = sb * cr + cb * sr

    grains_out = jnp.where(is_source, jnp.where(t == 0, 7, 8), 0)
    pl.semaphore_wait(bar, len(peers) + grains_out)

    rows128 = pl.ds(pl.multiple_of(mine * 128, 128), 128)
    rows16 = pl.ds(pl.multiple_of(mine * 16, 16), 16)
    my_block = core * 4 + b
    o_cols = pl.ds(pl.multiple_of(my_block * 512, 512), 512)
    quarter = pl.ds(pl.multiple_of(a * 128, 128), 128)
    k_zk, k_zv, k_zq, k_zo = sem(), sem(), sem(), sem()
    send(k_zk, wk_hbm.at[rows128], w_kv.at[slot, rows128, pl.ds(0, 128)], wpart)
    send(k_zv, wv_hbm.at[rows128], w_kv.at[slot, rows128, pl.ds(128, 128)], wpart)
    send(k_zq, wq_hbm.at[rows128], w_q.at[slot, my_block, quarter], wpart)
    send(k_zo, wo_hbm.at[quarter, o_cols], w_o.at[slot, my_block, quarter], wpart)

    x_load.wait()
    k_scat = [sem() for _ in range(8)]

    def grain_target(j):
        mm = 8 * parity + j
        aa = mm % 4
        bb = mm // 4
        return at(aa * (1 - slot) + bb * slot, bb * (1 - slot) + aa * slot, 0, t, slot)

    def grain_copy(j):
        return pltpu.make_async_remote_copy(
            src_ref=x_ref.at[pl.ds(16 * j, 16)], dst_ref=grain, send_sem=ss.at[k_scat[j]], recv_sem=rs.at[k_scat[0]],
            device_id=grain_target(j), device_id_type=MESH,
        )

    @pl.when(is_source)
    def _():
        for j in range(1, 8):
            grain_copy(j).start()

    @pl.when(is_source & (t != 0))
    def _():
        grain_copy(0).start()

    @pl.when(self_grain)
    def _():
        cp = pltpu.make_async_copy(x_ref.at[pl.ds(0, 16)], grain, ls.at[18])
        cp.start()
        cp.wait()

    def kv_one(c_, b_, a_):
        return w_kv.at[other, pl.ds(pl.multiple_of((c_ * 16 + b_ * 4 + a_) * 128, 128), 128)]

    def kv_block(c_, b_):
        return w_kv.at[other, pl.ds(pl.multiple_of((c_ * 4 + b_) * 512, 512), 512)]

    def an_one(c_, b_, a_):
        return anchor_kv.at[:, pl.ds(pl.multiple_of((c_ * 16 + b_ * 4 + a_) * 16, 16), 16)]

    def an_block(c_, b_):
        return anchor_kv.at[:, pl.ds(pl.multiple_of((c_ * 4 + b_) * 64, 64), 64)]

    class Gather:
        def __init__(self, one, block):
            self.one, self.block = one, block
            self.ka = [sem() for _ in range(3)] if one else []
            self.kb = [sem() for _ in range(3)]
            self.kd = [sem() for _ in range(4)]

        def send_a(self):
            v = self.one(core, b, a)
            for d in (1, 3, 2):
                send(self.ka[d - 1], v, v, ring_a(d))

        def wait_a(self):
            for d in (1, 3, 2):
                recv(self.ka[d - 1], self.one(core, b, (a + 4 - d) % 4), ring_a(4 - d))

        def send_b(self):
            v = self.block(core, b)
            for d in (1, 3, 2):
                send(self.kb[d - 1], v, v, ring_b(d))
            send(self.kd[0], v, v, sibling)

        def wait_b(self):
            for d in (1, 3, 2):
                v = self.block(core, (b + 4 - d) % 4)
                recv(self.kb[d - 1], v, ring_b(4 - d))
                send(self.kd[d], v, v, sibling)

        def wait_d(self):
            for d in (0, 1, 3, 2):
                recv(self.kd[d], self.block(1 - core, (a + 4 - d) % 4), sibling)

    class Stream:
        def __init__(self, block, pieces, slices):
            self.block, self.n, self.g = block, pieces, 512 // pieces
            self.ka = [sem() for _ in range(3)] if slices else []
            self.kb = [[sem() for _ in range(2)] for _ in range(pieces)]
            self.kc = [[sem() for _ in range(2)] for _ in range(pieces)]
            self.kd = [[sem() for _ in range(4)] for _ in range(pieces)]

        def piece(self, c_, b_, k):
            return self.block(c_, b_, pl.ds(k * self.g, self.g))

        def half(self, b_, k, h):
            return self.block(core, b_, pl.ds(k * self.g + h * (self.g // 2), self.g // 2))

        def one(self, a_):
            return self.block(core, b, pl.ds(pl.multiple_of(a_ * 128, 128), 128))

        def send_a(self):
            v = self.one(a)
            for d in (1, 3, 2):
                send(self.ka[d - 1], v, v, ring_a(d))

        def wait_a(self):
            for d in (1, 3, 2):
                recv(self.ka[d - 1], self.one((a + 4 - d) % 4), ring_a(4 - d))

        def first(self, k):
            v = self.piece(core, b, k)
            for i, d in enumerate((1, 3)):
                send(self.kb[k][i], v, v, ring_b(d))
            send(self.kd[k][0], v, v, sibling)

        def on(self, k):
            for i, d in enumerate((1, 3)):
                near = (b + 4 - d) % 4
                recv(self.kb[k][i], self.piece(core, near, k), ring_b(4 - d))
                v = self.half(near, k, i)
                send(self.kc[k][i], v, v, ring_b(d))
                v = self.piece(core, near, k)
                send(self.kd[k][d], v, v, sibling)

        def last(self, k):
            far_b = (b + 2) % 4
            for i, d in enumerate((1, 3)):
                recv(self.kc[k][i], self.half(far_b, k, i), ring_b(4 - d))
            v = self.piece(core, far_b, k)
            send(self.kd[k][2], v, v, sibling)

        def wait_d(self, ds=(0, 1, 3, 2)):
            for d in ds:
                for k in range(self.n):
                    recv(self.kd[k][d], self.piece(1 - core, (a + 4 - d) % 4, k), sibling)

    def q_view(c_, b_, rows):
        return w_q.at[other, c_ * 4 + b_, rows]

    def o_view(c_, b_, rows):
        return w_o.at[other, c_ * 4 + b_, rows]

    kv_gather = Gather(kv_one, kv_block)
    an_gather = Gather(None, an_block)
    q_str = Stream(q_view, 4, True)
    o_str = Stream(o_view, 2, True)

    def norm(rows):
        v = rows.astype(F32)
        mean_sq = jnp.mean(v * v, axis=-1, keepdims=True)
        return (v * lax.rsqrt(mean_sq + EPS) * gain_ref[...]).astype(BF16)

    k_norm = [sem() for _ in range(4)]
    for i in range(2):

        @pl.loop(0, 4)
        def _(r, i=i):
            rr = pl.ds(pl.multiple_of(i * 64 + r * 16, 16), 16)
            normed[rr] = norm(x_ref[rr])

        if i == 0:
            send(k_norm[0], normed.at[pl.ds(0, 32)], normed.at[pl.ds(192, 32)], below)
        else:
            send(k_norm[1], normed.at[pl.ds(64, 32)], normed.at[pl.ds(128, 32)], above)

    recv(k_zk, w_kv.at[other, rows128, pl.ds(0, 128)], wpart)
    recv(k_zv, w_kv.at[other, rows128, pl.ds(128, 128)], wpart)
    kv_gather.send_a()

    k_pair = sem()

    def grain_forward():
        return pltpu.make_async_remote_copy(
            src_ref=grain, dst_ref=grain, send_sem=ss.at[k_pair], recv_sem=rs.at[k_pair], device_id=pair, device_id_type=MESH
        )

    @pl.when(takes_first & jnp.logical_not(self_grain))
    def _():
        recv(k_scat[0], grain, (0, t))

    @pl.when(takes_first)
    def _():
        grain_forward().start()

    send(k_norm[2], normed.at[pl.ds(32, 32)], normed.at[pl.ds(224, 32)], below)
    send(k_norm[3], normed.at[pl.ds(96, 32)], normed.at[pl.ds(160, 32)], above)

    recv(k_zq, q_str.one(a), wpart)
    q_str.send_a()
    kv_gather.wait_a()
    kv_gather.send_b()
    recv(k_zo, o_str.one(a), wpart)
    o_str.send_a()
    table_load.wait()
    fill_tables(0, 128, pl.multiple_of(own_start, 128), offsets_ref[ctx])
    fill_tables(128, 64, pl.multiple_of(low_start, 64), offsets_ref[low_ctx])
    fill_tables(192, 64, pl.multiple_of(high_start, 64), offsets_ref[high_ctx])
    fill_tables(256, 16, pl.multiple_of(mine * 16, 16), offsets_ref[0])
    for cp in loads:
        cp.wait()

    def rope(v, c, s):
        return v * c + pltpu.roll(v, 64, 1) * s

    k_own = [sem() for _ in range(4)]
    k_low, k_high, k_high4 = sem(), sem(), sem()

    def kv_view(buf, i, start, n):
        return block_kv.at[buf, i, pl.ds(pl.multiple_of(start, 64), n)]

    def kv_send(k, src, dst, dev):
        return pltpu.make_async_remote_copy(
            src_ref=src, dst_ref=dst, send_sem=ss.at[k], recv_sem=rs.at[k], device_id=dev, device_id_type=MESH
        )

    both = pl.ds(0, 2)
    to_foreign = jnp.where(t == 2, 1, 0)

    def own_to_2(n, i):
        return kv_send(k_own[n], kv_view(0, i, own_start, 128), kv_view(to_foreign, i, own_start, 128), along_z(2))

    def own_to_4(n, i):
        return kv_send(k_own[2 + n], kv_view(0, i, 0, 128), kv_view(1, i, 0, 128), along_z(4))

    def low_to_2():
        return kv_send(k_low, kv_view(0, both, low_start, 64), kv_view(to_foreign, both, low_start, 64), along_z(2))

    def high_to_2():
        return kv_send(
            k_high, kv_view(high_foreign, both, high_start, 64), kv_view(to_foreign, both, high_start, 64), along_z(2)
        )

    def high_to_4():
        return kv_send(
            k_high4, kv_view(high_foreign, both, high_start, 64), kv_view(low_foreign, both, high_start, 64), along_z(4)
        )

    def kv_own(n, i):
        kv = jnp.dot(normed[pl.ds(0, 128)], w_kv[i], preferred_element_type=F32)
        rows = pl.ds(pl.multiple_of(own_start, 128), 128)
        block_kv[0, i, rows, pl.ds(0, 128)] = rope(kv[:, :128], cos_ref[pl.ds(0, 128)], sin_ref[pl.ds(0, 128)]).astype(BF16)
        block_kv[0, i, rows, pl.ds(128, 128)] = kv[:, 128:].astype(BF16)

        @pl.when(t <= 2)
        def _():
            own_to_2(n, i).start()

        @pl.when(t == 0)
        def _():
            own_to_4(n, i).start()

    def kv_near():
        for i in range(2):
            kv = jnp.dot(normed[pl.ds(128, 128)], w_kv[i], preferred_element_type=F32)
            key = rope(kv[:, :128], cos_ref[pl.ds(128, 128)], sin_ref[pl.ds(128, 128)]).astype(BF16)
            value = kv[:, 128:].astype(BF16)
            low_rows = pl.ds(pl.multiple_of(low_start, 64), 64)
            high_rows = pl.ds(pl.multiple_of(high_start, 64), 64)
            block_kv[low_foreign, i, low_rows, pl.ds(0, 128)] = key[:64]
            block_kv[low_foreign, i, low_rows, pl.ds(128, 128)] = value[:64]
            block_kv[high_foreign, i, high_rows, pl.ds(0, 128)] = key[64:]
            block_kv[high_foreign, i, high_rows, pl.ds(128, 128)] = value[64:]
        high_to_2().start()

        @pl.when((t == 1) | (t == 2))
        def _():
            low_to_2().start()

        @pl.when((t == 0) | (t == 3))
        def _():
            high_to_4().start()

    for n in range(4):

        @pl.when(t == n)
        def _(n=n):
            if n < 3:
                start = n * 128 + 192
                block_kv[0, :, pl.ds(start, 512 - start)] = jnp.zeros((2, 512 - start, 256), BF16)
            else:
                block_kv[1, :, pl.ds(64, 448)] = jnp.zeros((2, 448, 256), BF16)

    kv_own(0, slot)

    def q_rows(near, i):
        rows = pl.ds(near * 128, 128)

        @pl.loop(0, 2)
        def _(j):
            c = cos_ref[rows]
            s = sin_ref[rows]
            q = jnp.dot(
                normed[rows], w_q[i, :, :, pl.ds(pl.multiple_of(j * 256, 256), 256)].reshape(4096, 256),
                preferred_element_type=F32,
            )
            for h in range(2):
                v = rope(q[:, h * 128 : (h + 1) * 128], c, s).astype(BF16)
                if near:
                    place = pl.ds(pl.multiple_of((j * 2 + h) * 64, 64), 64)
                    q_near[i, 0, place] = v[:64]
                    q_near[i, 1, place] = v[64:]
                else:
                    q_own[i, j, pl.ds(h * 128, 128)] = v

    q_rows(0, slot)
    q_str.wait_a()
    q_str.first(0)
    q_str.first(1)
    q_str.first(2)
    q_str.first(3)
    kv_gather.wait_b()

    @pl.when(takes_second)
    def _():
        recv(k_pair, grain, pair)

    @pl.when(takes)
    def _():
        grain_norm[...] = norm(grain[...])

    kv_gather.wait_d()

    k_an = [sem() for _ in range(15)]
    k_an_in = [sem() for _ in range(4)]
    an_mine = an_one(core, b, a)
    zs, ds = (0, 2, 4, 6), (0, 1, 3, 2)

    def anchor_copy(n):
        dz, d = [(i, j) for j in ds for i in zs][1:][n]
        z = (zh * 4 + t + dz) % 8
        dev = at((x + d * (1 - core)) % 4, (y + d * core) % 4, z // 4, z % 4, core)
        return pltpu.make_async_remote_copy(
            src_ref=an_mine, dst_ref=an_mine, send_sem=ss.at[k_an[n]], recv_sem=rs.at[k_an_in[d]],
            device_id=dev, device_id_type=MESH,
        )

    @pl.when(takes)
    def _():
        c = cos_ref[pl.ds(256, 16)]
        s = sin_ref[pl.ds(256, 16)]
        for i in range(2):
            kv = jnp.dot(grain_norm[...], w_kv[i], preferred_element_type=F32)
            anchor_kv[i, rows16, pl.ds(0, 128)] = rope(kv[:, :128], c, s).astype(BF16)
            anchor_kv[i, rows16, pl.ds(128, 128)] = kv[:, 128:].astype(BF16)
        for i in range(15):
            anchor_copy(i).start()

    kv_own(1, other)
    q_str.on(0)
    q_str.on(1)
    recv(k_norm[0], normed.at[pl.ds(192, 32)], above)
    recv(k_norm[1], normed.at[pl.ds(128, 32)], below)
    recv(k_norm[2], normed.at[pl.ds(224, 32)], above)
    recv(k_norm[3], normed.at[pl.ds(160, 32)], below)
    kv_near()

    q_str.on(2)
    q_str.on(3)
    o_str.wait_a()
    o_str.first(0)
    o_str.first(1)
    q_rows(1, slot)

    @pl.when(jnp.logical_not(takes))
    def _():
        recv(k_an_in[0], an_mine, pair)

    for d in (1, 3, 2):
        recv(k_an_in[d], an_one(core, b, (a + 4 - d) % 4), pair)
    an_gather.send_b()
    q_str.last(0)
    q_str.last(1)
    q_str.last(2)
    q_str.last(3)
    an_gather.wait_b()
    q_str.wait_d()
    o_str.on(0)
    q_rows(1, other)
    o_str.on(1)
    an_gather.wait_d()

    @pl.when(t != 1)
    def _():
        for n in range(2):
            v = kv_view(low_foreign, n, (own_start + 256) % 512, 128)
            kv_send(k_own[n], v, v, along_z(6)).wait_recv()

    @pl.when((t == 0) | (t == 3))
    def _():
        v = kv_view(low_foreign, both, (low_start + 256) % 512, 64)
        kv_send(k_low, v, v, along_z(6)).wait_recv()
        v = kv_view(low_foreign, both, high_start, 64)
        kv_send(k_high4, v, v, along_z(4)).wait_recv()

    @pl.when(t == 0)
    def _():
        for n in range(2):
            v = kv_view(1, n, 0, 128)
            kv_send(k_own[2 + n], v, v, along_z(4)).wait_recv()

    v = kv_view(low_foreign, both, (high_start + 256) % 512, 64)
    recv(k_high, v, along_z(6))

    scale = LOG2_E / HD**0.5
    dims = (((1,), (1,)), ((), ()))

    def attend(q, i, buf, block, start, length):
        s1 = lax.dot_general(q, anchor_kv[i, :, pl.ds(0, 128)], dims, preferred_element_type=F32)
        s2 = lax.dot_general(q, block_kv[buf, i, :, pl.ds(0, 128)], dims, preferred_element_type=F32)
        qpos = start + lax.broadcasted_iota(jnp.int32, (256, 512), 0) % length
        kpos = lax.broadcasted_iota(jnp.int32, (256, 512), 1)
        s2 = jnp.where(kpos <= qpos, s2, NEG)
        hidden = jnp.where(block == 0, NEG, 0.0)
        top = jnp.maximum(jnp.max(s1, axis=-1, keepdims=True) + hidden, jnp.max(s2, axis=-1, keepdims=True))
        e1 = jnp.exp2((s1 - (top - hidden)) * scale)
        e2 = jnp.exp2((s2 - top) * scale)
        total = jnp.sum(e1, axis=-1, keepdims=True) + jnp.sum(e2, axis=-1, keepdims=True)
        o = jnp.dot(e1.astype(BF16), anchor_kv[i, :, pl.ds(128, 128)], preferred_element_type=F32)
        o += jnp.dot(e2.astype(BF16), block_kv[buf, i, :, pl.ds(128, 128)], preferred_element_type=F32)
        return (o / total).astype(BF16)

    @pl.loop(0, 2)
    def _(i):
        o = attend(q_near[i, 0], i, low_foreign, low_ctx, low_start, 64)
        for h in range(4):
            att_near[i, pl.ds(0, 64), pl.ds(h * 128, 128)] = o[h * 64 : (h + 1) * 64]
        o = attend(q_near[i, 1], i, high_foreign, high_ctx, high_start, 64)
        for h in range(4):
            att_near[i, pl.ds(64, 64), pl.ds(h * 128, 128)] = o[h * 64 : (h + 1) * 64]

    order = [core * 4 + b, (1 - core) * 4 + a]
    order += [core * 4 + (b + 3) % 4, core * 4 + (b + 1) % 4, (1 - core) * 4 + (a + 3) % 4, (1 - core) * 4 + (a + 1) % 4]
    order += [core * 4 + (b + 2) % 4, (1 - core) * 4 + (a + 2) % 4]
    k_sum = [(sem(), sem()) for _ in range(8)]
    lower, upper = pl.ds(0, 64), pl.ds(64, 64)

    def out_block(att, j):
        return jnp.dot(att[0], w_o[0, j], preferred_element_type=F32) + jnp.dot(att[1], w_o[1, j], preferred_element_type=F32)

    def send_sum(i):
        send_buf[i] = out_block(att_near, order[i]).astype(BF16)
        send(k_sum[i][0], send_buf.at[i, lower], recv_buf.at[i, upper], below)
        send(k_sum[i][1], send_buf.at[i, upper], recv_buf.at[i, lower], above)

    send_sum(0)
    o_str.wait_d((0,))
    send_sum(1)
    send_sum(2)
    send_sum(3)
    o_str.wait_d((1, 3))
    send_sum(4)
    send_sum(5)
    o_str.last(0)
    o_str.last(1)
    send_sum(6)
    o_str.wait_d((2,))
    send_sum(7)
    q_rows(0, other)

    @pl.loop(0, 4)
    def _(n):
        i = n // 2
        o = attend(q_own[i, n % 2], i, 0, ctx, own_start, 128)
        for h in range(2):
            att_own[i, :, pl.ds(pl.multiple_of((n % 2) * 256 + h * 128, 128), 128)] = o[h * 128 : (h + 1) * 128]

    @pl.loop(0, 8)
    def _(j):
        cols = pl.ds(pl.multiple_of(j * 512, 512), 512)
        partial[:, cols] = x_ref[:, cols].astype(F32) + out_block(att_own, j)

    @pl.when(is_source)
    def _():
        for j in range(1, 8):
            grain_copy(j).wait_send()

    @pl.when(is_source & (t != 0))
    def _():
        grain_copy(0).wait_send()

    @pl.when(takes_first)
    def _():
        grain_forward().wait_send()

    @pl.when(takes)
    def _():
        for i in range(15):
            anchor_copy(i).wait_send()

    @pl.when(t <= 2)
    def _():
        for n in range(2):
            own_to_2(n, n).wait_send()

    @pl.when(t == 0)
    def _():
        for n in range(2):
            own_to_4(n, n).wait_send()

    high_to_2().wait_send()

    @pl.when((t == 1) | (t == 2))
    def _():
        low_to_2().wait_send()

    @pl.when((t == 0) | (t == 3))
    def _():
        high_to_4().wait_send()

    for cp in sends[:-16]:
        cp.wait_send()
    stores = []
    for i in range(8):
        recv(k_sum[i][0], recv_buf.at[i, upper], above)
        recv(k_sum[i][1], recv_buf.at[i, lower], below)
        cols = pl.ds(pl.multiple_of(order[i] * 512, 512), 512)
        out_buf[i] = (partial[:, cols] + recv_buf[i].astype(F32)).astype(BF16)
        cp = pltpu.make_async_copy(out_buf.at[i], out_ref.at[:, cols], ls.at[i])
        cp.start()
        stores.append(cp)
    for cp in stores:
        cp.wait()
    for cp in sends[-16:]:
        cp.wait_send()
    assert count[0] <= N_SEM, count[0]


def angle_tables():
    freq = 500000.0 ** (-(np.arange(HD // 2) * 2.0 / HD))
    sign = np.concatenate([-np.ones(HD // 2), np.ones(HD // 2)])[None]

    def both(positions):
        angle = np.asarray(positions, np.float64)[:, None] * np.concatenate([freq, freq])[None]
        return np.cos(angle).astype(np.float32), (np.sin(angle) * sign).astype(np.float32)

    return np.stack(both(np.concatenate([np.arange(512), np.arange(128) * 512])))


def body(hidden_in, norm_gain, w_query, w_key, w_value, w_out, offsets):
    vmem = pl.BlockSpec(memory_space=pltpu.VMEM)
    hbm = pl.BlockSpec(memory_space=pl.ANY)
    return pl.pallas_call(
        kernel,
        out_shape=jax.ShapeDtypeStruct((128, 4096), BF16),
        in_specs=[pl.BlockSpec(memory_space=pltpu.SMEM), vmem] + [hbm] * 6,
        out_specs=hbm,
        scratch_shapes=[
            pltpu.VMEM((2, 8, 512, 512), BF16),
            pltpu.VMEM((2, 4096, 256), BF16),
            pltpu.VMEM((2, 8, 512, 512), BF16),
            pltpu.VMEM((256, 4096), BF16),
            pltpu.VMEM((16, 4096), BF16),
            pltpu.VMEM((16, 4096), BF16),
            pltpu.VMEM((2, 512, 256), BF16),
            pltpu.VMEM((2, 2, 512, 256), BF16),
            pltpu.VMEM((2, 2, 256, 128), BF16),
            pltpu.VMEM((2, 2, 256, 128), BF16),
            pltpu.VMEM((2, 128, 512), BF16),
            pltpu.VMEM((2, 128, 512), BF16),
            pltpu.VMEM((8, 128, 512), BF16),
            pltpu.VMEM((8, 128, 512), BF16),
            pltpu.VMEM((128, 4096), F32),
            pltpu.VMEM((272, 128), F32),
            pltpu.VMEM((272, 128), F32),
            pltpu.VMEM((128, 4096), BF16),
            pltpu.VMEM((2, 640, 128), F32),
            pltpu.VMEM((8, 128, 512), BF16),
            pltpu.SemaphoreType.DMA((N_SEM,)),
            pltpu.SemaphoreType.DMA((N_SEM,)),
            pltpu.SemaphoreType.DMA((21,)),
        ],
        compiler_params=pltpu.CompilerParams(collective_id=0, has_side_effects=True, vmem_limit_bytes=56 * 2**20),
        cost_estimate=pl.CostEstimate(flops=10**10, bytes_accessed=2 * 10**7, transcendentals=2 * 10**6),
    )(offsets, norm_gain.reshape(1, 4096), hidden_in, angle_tables(), w_query, w_key, w_value, w_out)


def solution(mesh):
    placed = (
        P(("context", "tensor"), None),
        P(),
        P(None, "tensor"),
        P(None, "tensor"),
        P(None, "tensor"),
        P("tensor", None),
        P(),
    )
    return jax.shard_map(
        body, mesh=mesh, in_specs=placed, out_specs=P(("context", "tensor"), None), check_vma=False
    )
```
